32 devices in a mesh: span: 8 (over y, x, core), space: 4 (over z).
Axes of the slice: x: 2, y: 2, z: 4, core: 2. Of those that a mesh axis runs over, the one named last changes fastest.
Arguments:
- latents: bfloat16 [96, 16, 3072], P('space', 'span'), may hold values from -6 to 6
- span_order: int32 [16], replicated, may hold values from 0 to 15, each once
- modulation: float32 [16, 6, 3072], P('span'), may hold values from -2 to 10
- qkv_weight: bfloat16 [3, 3072, 2048], P(None, None, 'space'), may hold values from -0.109375 to 0.109375
- out_weight: bfloat16 [2048, 3072], P('space'), may hold values from -0.125 to 0.125
- up_weight: bfloat16 [3072, 12288], P(None, 'space'), may hold values from -0.109375 to 0.109375
- down_weight: bfloat16 [12288, 3072], P('space'), may hold values from -0.0546875 to 0.0546875
Outputs:
- mixed: bfloat16 [96, 16, 3072], P('space', 'span')
The draws below stay inside these ranges and needn't reach their ends.
Inputs may be any that keep to these rules, and one draw needn't show every extreme that they name: `span_order`: a permutation of the span places 0 to 15.
All inputs are finite; a program needn't handle non-finite values.
Results may differ from the reference program's by a relative error of at most 0.025.
The reference program's roundings to bfloat16 on the way count: a program that leaves them out, or rounds other values in their place, can miss the bound.
Values may be sent and summed in bfloat16 or wider, within the bound.
A program may use at most 192 MiB of HBM per device.

```python
import jax
import jax.numpy as jnp
from jax import lax

D = 3072
HEADS = 16
HD = 128
FF = 12288
SPAN_TOK = 96
SPANS = 16
N_SPACE = 4


def draw_modulation(key, part):
    key = jax.random.fold_in(key, 11)
    first, second, third = jax.random.split(key, 3)
    shift = jnp.clip(jax.random.normal(first, (SPANS, 2, D), jnp.float32) * 0.5, -2.0, 2.0)
    scale = jax.random.uniform(second, (SPANS, 2, D), jnp.float32, -0.5, 1.0)
    gate = jax.random.uniform(third, (SPANS, 2, D), jnp.float32, 0.5, 1.5)
    return jnp.stack([shift[:, 0], scale[:, 0], gate[:, 0], shift[:, 1], scale[:, 1], gate[:, 1]], axis=1)


def level_of(own_key, dims, cuts, smallest, top_value):
    def one(axis_at, parts):
        draws = jax.random.uniform(jax.random.fold_in(jax.random.fold_in(own_key, 6), axis_at), (parts,), jnp.float32, smallest / len(cuts), top_value / len(cuts))
        return jnp.repeat(jnp.exp(draws), dims[axis_at] // parts).reshape((-1,) + (1,) * (len(dims) - axis_at - 1))

    gain = one(*cuts[0])
    for cut in cuts[1:]:
        gain = gain * one(*cut)
    return gain


def normal_values(rng, shape, scale, reach, shards=(), dtype=jnp.bfloat16):
    entries = scale * jax.random.normal(rng, shape, jnp.float32)
    if shards:
        entries = entries * level_of(rng, shape, shards, -0.22, 0.18)
    return jnp.clip(entries, -reach, reach).astype(dtype)


def setup_inputs(seed: int = 0) -> dict:
    key_list = jax.random.split(jax.random.key(seed), 8)
    latents = normal_values(key_list[0], (SPAN_TOK, SPANS, D), 1.0, 6.0, ((0, 4), (1, 8)))
    span_order = jax.random.permutation(key_list[1], SPANS).astype(jnp.int32)
    modulation = draw_modulation(jax.random.fold_in(key_list[7], 71), 0)
    qkv_weight = normal_values(key_list[3], (3, D, HEADS * HD), D ** -0.5, 0.109375, ((2, 4),))
    out_weight = normal_values(key_list[4], (HEADS * HD, D), (HEADS * HD) ** -0.5, 0.125, ((0, 4),))
    up_weight = normal_values(key_list[5], (D, FF), D ** -0.5, 0.109375, ((1, 4),))
    down_weight = normal_values(key_list[6], (FF, D), FF ** -0.5, 0.0546875, ((0, 4),))
    return {"latents": latents, "span_order": span_order, "modulation": modulation, "qkv_weight": qkv_weight, "out_weight": out_weight, "up_weight": up_weight, "down_weight": down_weight}


def norm_mod(rows, shift, scale):
    mean = lax.optimization_barrier(jnp.mean(rows, axis=-1, keepdims=True))
    centred = rows - mean
    variance = lax.optimization_barrier(jnp.mean(centred * centred, axis=-1, keepdims=True))
    return (centred * lax.rsqrt(variance + 1e-06) * (1.0 + scale) + shift).astype(jnp.bfloat16)

def grouped_sum(left, right, groups):
    width = left.shape[1] // groups
    total = jnp.zeros((left.shape[0], right.shape[1]), jnp.float32)
    for group in range(groups):
        part = jnp.dot(left[:, group * width:(group + 1) * width], right[group * width:(group + 1) * width], preferred_element_type=jnp.float32)
        total = total + lax.optimization_barrier(part.astype(jnp.bfloat16)).astype(jnp.float32)
    return total

def reference(latents, span_order, modulation, qkv_weight, out_weight, up_weight, down_weight):
    rows_f = latents.astype(jnp.float32)
    normed = norm_mod(rows_f, modulation[None, :, 0], modulation[None, :, 1])
    projected = jnp.einsum('tcd,sdf->stcf', normed.astype(jnp.float32), qkv_weight.astype(jnp.float32)).astype(jnp.bfloat16)
    per_head = projected.reshape(3, SPAN_TOK, SPANS, HEADS, HD).transpose(3, 0, 2, 1, 4)
    factor = 1.0 / HD ** 0.5

    def one_head(stacked):
        query = stacked[0].astype(jnp.float32)
        keys = stacked[1].astype(jnp.float32)
        values = stacked[2].astype(jnp.float32)

        def one_span(item):
            block, place = item
            scores = jnp.einsum('td,bud->tbu', block, keys) * factor
            allowed = (span_order <= place)[None, :, None]
            scores = jnp.where(allowed, scores, -1e+30)
            peak = lax.optimization_barrier(jnp.max(scores, axis=(1, 2), keepdims=True))
            expo = jnp.where(allowed, jnp.exp(scores - peak), 0.0)
            total = lax.optimization_barrier(jnp.sum(expo, axis=(1, 2)))
            weights = expo.astype(jnp.bfloat16).astype(jnp.float32)
            return jnp.einsum('tbu,bud->td', weights, values) / total[:, None]
        return lax.map(one_span, (query, span_order))
    heads_out = lax.map(one_head, per_head)
    attended = heads_out.transpose(2, 1, 0, 3).reshape(SPAN_TOK * SPANS, HEADS * HD).astype(jnp.bfloat16)
    attn_sum = grouped_sum(attended, out_weight, N_SPACE).reshape(SPAN_TOK, SPANS, D)
    residual = (rows_f + modulation[None, :, 2] * attn_sum).astype(jnp.bfloat16)
    second = norm_mod(residual.astype(jnp.float32), modulation[None, :, 3], modulation[None, :, 4])
    hidden = jax.nn.gelu(jnp.dot(second.reshape(-1, D), up_weight, preferred_element_type=jnp.float32), approximate=True).astype(jnp.bfloat16)
    ffn_sum = grouped_sum(hidden, down_weight, N_SPACE).reshape(SPAN_TOK, SPANS, D)
    return (residual.astype(jnp.float32) + modulation[None, :, 5] * ffn_sum).astype(jnp.bfloat16)
```

```python
import functools

import jax
import jax.numpy as jnp
from jax import lax
from jax.experimental import pallas as pl
from jax.experimental.pallas import tpu as pltpu
from jax.sharding import PartitionSpec as P

HD = 128
CHUNKS = 4
BLOCK = 512
MESH = pl.DeviceIdType.MESH
VMEM_BYTES = 62 * 1024 * 1024


def norm_mod(rows, shift, scale):
    mean = jnp.mean(rows, axis=-1, keepdims=True)
    centred = rows - mean
    variance = jnp.mean(centred * centred, axis=-1, keepdims=True)
    return (centred * lax.rsqrt(variance + 1e-06) * (1.0 + scale) + shift).astype(jnp.bfloat16)


def plain_body(latents, span_order, modulation, qkv_weight, out_weight, up_weight, down_weight):
    span_count = latents.shape[1]
    head_count = qkv_weight.shape[2] // HD
    my_start = lax.axis_index("span") * span_count
    my_places = lax.dynamic_slice_in_dim(span_order, my_start, span_count, 0)
    gathered = lax.all_gather(latents, "space", axis=0, tiled=True)
    group_rows = gathered.shape[0]
    gathered_f = gathered.astype(jnp.float32)
    normed = norm_mod(gathered_f, modulation[None, :, 0], modulation[None, :, 1])
    projected = jnp.einsum(
        "tcd,sdf->stcf", normed, qkv_weight, preferred_element_type=jnp.float32
    ).astype(jnp.bfloat16)
    query = projected[0].reshape(group_rows, span_count, head_count, HD)
    factor = 1.0 / HD**0.5
    running = jnp.full((head_count, span_count, group_rows), -1e30, jnp.float32)
    key_piece = lax.all_gather(projected[1], "span", axis=1, tiled=True)
    value_piece = lax.all_gather(projected[2], "span", axis=1, tiled=True)
    piece_spans = key_piece.shape[1]
    key_four = key_piece.reshape(group_rows, piece_spans, head_count, HD)
    value_four = value_piece.reshape(group_rows, piece_spans, head_count, HD)
    allowed = (span_order[None, :] <= my_places[:, None])[None, :, None, :, None]
    scores = (
        jnp.einsum("tahd,ubhd->hatbu", query, key_four, preferred_element_type=jnp.float32) * factor
    )
    scores = jnp.where(allowed, scores, -1e30)
    newest = jnp.maximum(running, jnp.max(scores, axis=(3, 4)))
    expo = jnp.where(allowed, jnp.exp(scores - newest[..., None, None]), 0.0)
    denom = jnp.sum(expo, axis=(3, 4))
    accum = jnp.einsum(
        "hatbu,ubhd->hatd",
        expo.astype(jnp.bfloat16),
        value_four,
        preferred_element_type=jnp.float32,
    )
    running, denom, accum = (newest, denom, accum)
    attended = (
        (accum / denom[..., None])
        .transpose(2, 1, 0, 3)
        .reshape(group_rows, span_count, head_count * HD)
        .astype(jnp.bfloat16)
    )
    rows = attended
    attn_sum = lax.psum_scatter(
        jnp.einsum("tck,kd->tcd", rows, out_weight, preferred_element_type=jnp.float32).astype(
            jnp.bfloat16
        ),
        "space",
        scatter_dimension=0,
        tiled=True,
    ).astype(jnp.float32)
    residual = (latents.astype(jnp.float32) + modulation[None, :, 2] * attn_sum).astype(
        jnp.bfloat16
    )
    second = norm_mod(
        lax.all_gather(residual, "space", axis=0, tiled=True).astype(jnp.float32),
        modulation[None, :, 3],
        modulation[None, :, 4],
    )
    hidden = jax.nn.gelu(
        jnp.einsum("tcd,df->tcf", second, up_weight, preferred_element_type=jnp.float32),
        approximate=True,
    ).astype(jnp.bfloat16)
    rows = hidden
    ffn_sum = lax.psum_scatter(
        jnp.einsum("tcf,fd->tcd", rows, down_weight, preferred_element_type=jnp.float32).astype(
            jnp.bfloat16
        ),
        "space",
        scatter_dimension=0,
        tiled=True,
    ).astype(jnp.float32)
    return (residual.astype(jnp.float32) + modulation[None, :, 5] * ffn_sum).astype(jnp.bfloat16)


def flip(index, bit):
    return index + bit * (1 - 2 * ((index // bit) % 2))


def layer_kernel(
    nz, ns, span_count, order_ref, key_order_ref, x_ref, mod_ref, qkv_hbm, out_hbm, up_hbm, down_hbm,
    mixed_ref,
    w_a, w_b, w_out, w_up, gathered, normed, query, kv, expo, scores, denom, attended, part,
    from_left, from_right, from_left2, from_right2, resid, hidden, acc,
    w_sem, ag_send, ag_recv, kv_send, kv_recv, rs_send, rs_recv,
):
    z = lax.axis_index("space")
    me = lax.axis_index("span")
    rows, width = x_ref.shape
    tok = rows // span_count
    wide = width // CHUNKS
    last = nz - 1
    heads = query.shape[1] // HD
    down_blocks = width // BLOCK
    first_blocks = w_b.shape[0]

    def load(src, dst, slot):
        return pltpu.make_async_copy(src, dst, w_sem.at[slot])

    def columns(c, size):
        return pl.ds(c * size, size)

    qkv_loads = [load(qkv_hbm.at[i], w_a.at[i], i) for i in range(3)]
    out_load = load(out_hbm, w_out, 3)
    up_loads = [load(up_hbm.at[:, columns(i, BLOCK)], w_up.at[i], 4 + i) for i in range(w_up.shape[0])]
    down_base = 4 + w_up.shape[0]
    down_loads = [
        load(
            down_hbm.at[:, columns(i, BLOCK)],
            w_b.at[i] if i < first_blocks else w_a.at[i - first_blocks],
            down_base + i,
        )
        for i in range(down_blocks)
    ]
    for i in (1, 2, 0):
        qkv_loads[i].start()

    barrier = pltpu.get_barrier_semaphore()
    for bit in (1, 2, 4):
        pl.semaphore_signal(barrier, inc=1, device_id=(flip(me, bit), z), device_id_type=MESH)

    @pl.when(z > 0)
    def _():
        pl.semaphore_signal(barrier, inc=1, device_id=(me, z - 1), device_id_type=MESH)

    @pl.when(z < last)
    def _():
        pl.semaphore_signal(barrier, inc=1, device_id=(me, z + 1), device_id_type=MESH)

    pl.semaphore_wait(barrier, 3 + jnp.where(z > 0, 1, 0) + jnp.where(z < last, 1, 0))

    def ag_copy(which, way, s, c, src, dst):
        return pltpu.make_async_remote_copy(
            src_ref=src, dst_ref=dst,
            send_sem=ag_send.at[which, way, s, c], recv_sem=ag_recv.at[which, way, s, c],
            device_id=(me, z + 1 if way == 0 else z - 1), device_id_type=MESH,
        )

    def ag_sends(way, s):
        return jnp.logical_and(z < last, z - s >= 0) if way == 0 else jnp.logical_and(z > 0, z + s <= last)

    def ag_gets(way, s):
        return z - 1 - s >= 0 if way == 0 else z + 1 + s <= last

    def ag_own(which, own, buf, c):
        for way in range(2):
            @pl.when(ag_sends(way, 0))
            def _():
                ag_copy(which, way, 0, c, own.at[:, columns(c, wide)], buf.at[z, :, columns(c, wide)]).start()

    def ag_step(which, buf, s, c):
        for way in range(2):
            block = z - 1 - s if way == 0 else z + 1 + s

            @pl.when(ag_gets(way, s))
            def _():
                piece = buf.at[block, :, columns(c, wide)]
                ag_copy(which, way, s, c, piece, piece).wait_recv()

            if s + 1 < last:
                @pl.when(ag_sends(way, s + 1))
                def _():
                    piece = buf.at[block, :, columns(c, wide)]
                    ag_copy(which, way, s + 1, c, piece, piece).start()

    def ag_drain(which, buf):
        for way in range(2):
            for s in range(last):
                for c in range(CHUNKS):
                    @pl.when(ag_sends(way, s))
                    def _():
                        piece = buf.at[0, :, columns(c, wide)]
                        ag_copy(which, way, s, c, piece, piece).wait_send()

    def norm_block(block, first):
        r = block.astype(jnp.float32)
        centred = r - jnp.mean(r, axis=-1, keepdims=True)
        variance = jnp.mean(centred * centred, axis=-1, keepdims=True)
        y = centred * lax.rsqrt(variance + 1e-06)
        pieces = []
        for a in range(span_count):
            shift = mod_ref[a, first : first + 1, :]
            scale = mod_ref[a, first + 1 : first + 2, :]
            pieces.append(y[a * tok : (a + 1) * tok] * (1.0 + scale) + shift)
        return jnp.concatenate(pieces, axis=0).astype(jnp.bfloat16)

    for c in range(CHUNKS):
        ag_own(0, x_ref, gathered, c)
    out_load.start()
    for copy in up_loads:
        copy.start()
    for copy in down_loads[:first_blocks]:
        copy.start()
    normed[z] = norm_block(x_ref[...], 0)
    for s in range(last):
        for c in range(CHUNKS):
            ag_step(0, gathered, s, c)
        for way in range(2):
            @pl.when(ag_gets(way, s))
            def _():
                block = z - 1 - s if way == 0 else z + 1 + s
                normed[block] = norm_block(gathered[block], 0)

    def kv_copy(which, rel, bit):
        piece = kv.at[which, flip_all(me, rel ^ bit)]
        return pltpu.make_async_remote_copy(
            src_ref=piece, dst_ref=piece,
            send_sem=kv_send.at[which, rel], recv_sem=kv_recv.at[which, rel],
            device_id=(flip(me, bit), z), device_id_type=MESH,
        )

    def flip_all(index, rel):
        for bit in (1, 2, 4):
            if rel & bit:
                index = flip(index, bit)
        return index

    def kv_take(which, rel):
        piece = kv.at[which, flip_all(me, rel)]
        pltpu.make_async_remote_copy(
            src_ref=piece, dst_ref=piece,
            send_sem=kv_send.at[which, rel], recv_sem=kv_recv.at[which, rel],
            device_id=(flip(me, 1), z), device_id_type=MESH,
        ).wait_recv()

    total_rows = nz * rows

    def project(i):
        qkv_loads[i].wait()
        return jnp.dot(
            normed[...].reshape(total_rows, width), w_a[i], preferred_element_type=jnp.float32
        ).astype(jnp.bfloat16)

    kv[0, me] = project(1)
    kv_copy(0, 2, 2).start()
    kv_copy(0, 4, 4).start()
    kv_copy(0, 1, 1).start()
    kv[1, me] = project(2)
    kv_copy(1, 4, 4).start()
    kv_copy(1, 2, 2).start()
    kv_copy(1, 1, 1).start()
    query[...] = project(0)
    for copy in down_loads[first_blocks:]:
        copy.start()
    ag_drain(0, gathered)
    kv_take(0, 2)
    kv_copy(0, 6, 4).start()
    kv_copy(0, 3, 1).start()
    kv_take(0, 4)
    kv_copy(0, 5, 1).start()
    kv_take(1, 4)
    kv_copy(1, 6, 2).start()
    kv_copy(1, 5, 1).start()
    kv_take(1, 2)
    kv_copy(1, 3, 1).start()
    kv_take(0, 6)
    kv_copy(0, 7, 1).start()
    for rel in (1, 3, 5, 7):
        kv_take(0, rel)

    keys_rows = ns * total_rows
    factor = 1.0 / HD**0.5
    places = [order_ref[me * span_count + a] for a in range(span_count)]

    def head_scores(h):
        lanes = pl.ds(pl.multiple_of(h * HD, HD), HD)
        keys = kv[0, :, :, lanes].reshape(keys_rows, HD)
        scores[...] = lax.dot_general(
            query[:, lanes], keys, (((1,), (1,)), ((), ())), preferred_element_type=jnp.float32
        )
        key_order = key_order_ref[...]
        for block in range(nz):
            out = []
            sums = []
            for a in range(span_count):
                at = block * rows + a * tok
                allowed = key_order <= places[a]
                sc = jnp.where(allowed, scores[at : at + tok, :] * factor, -1e30)
                e = jnp.exp(sc - jnp.max(sc, axis=-1, keepdims=True))
                e = jnp.where(allowed, e, 0.0)
                out.append(e)
                sums.append(jnp.broadcast_to(jnp.sum(e, axis=-1, keepdims=True), (tok, HD)))
            expo[h, block * rows : (block + 1) * rows, :] = jnp.concatenate(out, axis=0).astype(jnp.bfloat16)
            denom[h, block * rows : (block + 1) * rows, :] = jnp.concatenate(sums, axis=0)

    half = heads // 2

    @pl.loop(0, half)
    def _(h):
        head_scores(h)

    kv_take(1, 6)
    kv_copy(1, 7, 1).start()

    @pl.loop(half, heads)
    def _(h):
        head_scores(h)

    for rel in (1, 3, 5, 7):
        kv_take(1, rel)

    @pl.loop(0, heads)
    def _(h):
        lanes = pl.ds(pl.multiple_of(h * HD, HD), HD)
        mixed_values = jnp.dot(
            expo[h], kv[1, :, :, lanes].reshape(keys_rows, HD), preferred_element_type=jnp.float32
        )
        attended[:, lanes] = (mixed_values / denom[h]).astype(jnp.bfloat16)

    for which in range(2):
        for rel in range(1, 8):
            kv_copy(which, rel, rel & -rel if rel != 6 else (4 if which == 0 else 2)).wait_send()

    def rs_copy(which, way, s, c, owner):
        buf = ((from_left, from_right), (from_left2, from_right2))[which][way]
        return pltpu.make_async_remote_copy(
            src_ref=part.at[owner, :, columns(c, wide)], dst_ref=buf.at[owner, :, columns(c, wide)],
            send_sem=rs_send.at[which, way, s, c], recv_sem=rs_recv.at[which, way, s, c],
            device_id=(me, z + 1 if way == 0 else z - 1), device_id_type=MESH,
        )

    def rs_start(which, c):
        @pl.when(z == 0)
        def _():
            for s in range(last):
                rs_copy(which, 0, s, c, last - s).start()

        @pl.when(z == last)
        def _():
            for s in range(last):
                rs_copy(which, 1, s, c, s).start()

    def rs_pass(which, c):
        for s in range(last):
            for way in range(2):
                owner = last - s if way == 0 else s
                on = jnp.logical_and(z > 0, owner > z) if way == 0 else jnp.logical_and(z < last, owner < z)

                @pl.when(on)
                def _():
                    copy = rs_copy(which, way, s, c, owner)
                    copy.wait_recv()
                    buf = ((from_left, from_right), (from_left2, from_right2))[which][way]
                    at = columns(c, wide)
                    part[owner, :, at] = (
                        part[owner, :, at].astype(jnp.float32) + buf[owner, :, at].astype(jnp.float32)
                    ).astype(jnp.bfloat16)
                    copy.start()

        acc[...] = part[z, :, columns(c, wide)].astype(jnp.float32)

        @pl.when(z > 0)
        def _():
            rs_copy(which, 0, last - z, c, z).wait_recv()
            buf = (from_left, from_left2)[which]
            acc[...] += buf[z, :, columns(c, wide)].astype(jnp.float32)

        @pl.when(z < last)
        def _():
            rs_copy(which, 1, z, c, z).wait_recv()
            buf = (from_right, from_right2)[which]
            acc[...] += buf[z, :, columns(c, wide)].astype(jnp.float32)

    def rs_drain(which):
        for s in range(last):
            for way in range(2):
                owner = last - s if way == 0 else s
                for c in range(CHUNKS):
                    @pl.when(owner > z if way == 0 else owner < z)
                    def _():
                        rs_copy(which, way, s, c, owner).wait_send()

    def gated(base, gate, c):
        pieces = []
        for a in range(span_count):
            span_rows = slice(a * tok, (a + 1) * tok)
            factor_row = mod_ref[a, gate : gate + 1, columns(c, wide)]
            pieces.append(base[span_rows] + factor_row * acc[span_rows, :])
        return jnp.concatenate(pieces, axis=0).astype(jnp.bfloat16)

    out_load.wait()
    for c in range(CHUNKS):
        part[:, :, columns(c, wide)] = (
            jnp.dot(attended[...], w_out[:, columns(c, wide)], preferred_element_type=jnp.float32)
            .astype(jnp.bfloat16)
            .reshape(nz, rows, wide)
        )
        rs_start(0, c)
    for c in range(CHUNKS + last - 1):
        if c < CHUNKS:
            at = columns(c, wide)
            rs_pass(0, c)
            resid[z, :, at] = gated(x_ref[:, at].astype(jnp.float32), 2, c)
            ag_own(1, resid.at[z], resid, c)
        for s in range(last - 1):
            if 0 <= c - 1 - s < CHUNKS:
                ag_step(1, resid, s, c - 1 - s)
    rs_drain(0)
    for c in range(CHUNKS):
        ag_step(1, resid, last - 1, c)

    @pl.loop(0, nz)
    def _(block):
        normed[block] = norm_block(resid[block], 3)

    for copy in up_loads:
        copy.wait()

    @pl.loop(0, w_up.shape[0])
    def _(i):
        raised = jnp.dot(
            normed[...].reshape(total_rows, width), w_up[i], preferred_element_type=jnp.float32
        )
        hidden[:, pl.ds(pl.multiple_of(i * BLOCK, BLOCK), BLOCK)] = jax.nn.gelu(
            raised, approximate=True
        ).astype(jnp.bfloat16)

    ag_drain(1, resid)
    done = 0
    for i in range(down_blocks):
        down_loads[i].wait()
        weight = w_b[i] if i < first_blocks else w_a[i - first_blocks]
        part[:, :, columns(i, BLOCK)] = (
            jnp.dot(hidden[...], weight, preferred_element_type=jnp.float32)
            .astype(jnp.bfloat16)
            .reshape(nz, rows, BLOCK)
        )
        while done < CHUNKS and (done + 1) * wide <= (i + 1) * BLOCK:
            rs_start(1, done)
            done += 1
    for c in range(CHUNKS):
        at = columns(c, wide)
        rs_pass(1, c)
        mixed_ref[:, at] = gated(resid[z, :, at].astype(jnp.float32), 5, c)
    rs_drain(1)


def kernel_body(nz, ns, latents, span_order, modulation, qkv_weight, out_weight, up_weight, down_weight):
    tok, span_count, width = latents.shape
    rows = tok * span_count
    total = rows * nz
    head_cols = qkv_weight.shape[2]
    heads = head_cols // HD
    hid = up_weight.shape[1]
    keys_rows = ns * total
    x = latents.transpose(1, 0, 2).reshape(rows, width)
    key_order = jnp.broadcast_to(
        span_order.reshape(ns, 1, span_count, 1), (ns, nz, span_count, tok)
    ).reshape(1, keys_rows)
    blocks = width // BLOCK
    later = qkv_weight.shape[0]
    bf, f32 = jnp.bfloat16, jnp.float32
    vmem = pl.BlockSpec(memory_space=pltpu.VMEM)
    hbm = pl.BlockSpec(memory_space=pl.ANY)
    grouped = pltpu.VMEM((nz, rows, width), bf)
    flops = 2 * total * width * (4 * head_cols + 2 * hid) + 4 * total * keys_rows * head_cols
    mixed = pl.pallas_call(
        functools.partial(layer_kernel, nz, ns, span_count),
        out_shape=jax.ShapeDtypeStruct((rows, width), bf),
        in_specs=[pl.BlockSpec(memory_space=pltpu.SMEM), vmem, vmem, vmem, hbm, hbm, hbm, hbm],
        out_specs=vmem,
        scratch_shapes=[
            pltpu.VMEM((later, width, head_cols), bf),
            pltpu.VMEM((blocks - later, hid, BLOCK), bf),
            pltpu.VMEM((head_cols, width), bf),
            pltpu.VMEM((hid // BLOCK, width, BLOCK), bf),
            grouped,
            grouped,
            pltpu.VMEM((total, head_cols), bf),
            pltpu.VMEM((2, ns, total, head_cols), bf),
            pltpu.VMEM((heads, total, keys_rows), bf),
            pltpu.VMEM((total, keys_rows), f32),
            pltpu.VMEM((heads, total, HD), f32),
            pltpu.VMEM((total, head_cols), bf),
            grouped,
            grouped,
            grouped,
            grouped,
            grouped,
            grouped,
            pltpu.VMEM((total, hid), bf),
            pltpu.VMEM((rows, width // CHUNKS), f32),
            pltpu.SemaphoreType.DMA((4 + hid // BLOCK + blocks,)),
            pltpu.SemaphoreType.DMA((2, 2, nz - 1, CHUNKS)),
            pltpu.SemaphoreType.DMA((2, 2, nz - 1, CHUNKS)),
            pltpu.SemaphoreType.DMA((2, ns)),
            pltpu.SemaphoreType.DMA((2, ns)),
            pltpu.SemaphoreType.DMA((2, 2, nz - 1, CHUNKS)),
            pltpu.SemaphoreType.DMA((2, 2, nz - 1, CHUNKS)),
        ],
        compiler_params=pltpu.CompilerParams(
            collective_id=0, has_side_effects=True, vmem_limit_bytes=VMEM_BYTES
        ),
        cost_estimate=pl.CostEstimate(
            flops=flops,
            bytes_accessed=2 * width * (4 * head_cols + 2 * hid),
            transcendentals=total * (keys_rows * heads + hid),
        ),
    )(span_order, key_order, x, modulation, qkv_weight, out_weight, up_weight, down_weight)
    return mixed.reshape(span_count, tok, width).transpose(1, 0, 2)


def fits(nz, ns, tok, span_count, width, head_cols, hid):
    rows = tok * span_count
    total = rows * nz
    keys_rows = ns * total
    weights = 2 * width * (4 * head_cols + 2 * hid) - 2 * width * 3 * head_cols
    moving = 2 * (9 * total * width + 2 * (keys_rows + total) * head_cols)
    moving += 2 * total * keys_rows * (head_cols // HD + 2) + 4 * total * head_cols
    return (
        ns == 8
        and nz > 1
        and rows % 16 == 0
        and tok % 8 == 0
        and head_cols == BLOCK
        and width == hid
        and width % BLOCK == 0
        and width % (CHUNKS * HD) == 0
        and weights + moving < VMEM_BYTES
    )


def body(nz, ns, latents, span_order, modulation, qkv_weight, out_weight, up_weight, down_weight):
    args = (latents, span_order, modulation, qkv_weight, out_weight, up_weight, down_weight)
    if fits(nz, ns, *latents.shape, qkv_weight.shape[2], up_weight.shape[1]):
        return kernel_body(nz, ns, *args)
    return plain_body(*args)


def solution(mesh):
    return jax.shard_map(
        functools.partial(body, mesh.shape["space"], mesh.shape["span"]),
        mesh=mesh,
        in_specs=(
            P("space", "span", None),
            P(),
            P("span", None, None),
            P(None, None, "space"),
            P("space", None),
            P(None, "space"),
            P("space", None),
        ),
        out_specs=P("space", "span", None),
        check_vma=False,
    )
```

```python
import functools

import jax
import jax.numpy as jnp
import numpy as np
from jax import lax
from jax.experimental import pallas as pl
from jax.experimental.pallas import tpu as pltpu
from jax.sharding import PartitionSpec as P

HD = 128
CHUNKS = 4
BLOCK = 512
MESH = pl.DeviceIdType.MESH
VMEM_BYTES = 62 * 1024 * 1024


def norm_mod(rows, shift, scale):
    mean = jnp.mean(rows, axis=-1, keepdims=True)
    centred = rows - mean
    variance = jnp.mean(centred * centred, axis=-1, keepdims=True)
    return (centred * lax.rsqrt(variance + 1e-06) * (1.0 + scale) + shift).astype(jnp.bfloat16)


def plain_body(latents, span_order, modulation, qkv_weight, out_weight, up_weight, down_weight):
    span_count = latents.shape[1]
    head_count = qkv_weight.shape[2] // HD
    my_start = lax.axis_index("span") * span_count
    my_places = lax.dynamic_slice_in_dim(span_order, my_start, span_count, 0)
    gathered = lax.all_gather(latents, "space", axis=0, tiled=True)
    group_rows = gathered.shape[0]
    gathered_f = gathered.astype(jnp.float32)
    normed = norm_mod(gathered_f, modulation[None, :, 0], modulation[None, :, 1])
    projected = jnp.einsum(
        "tcd,sdf->stcf", normed, qkv_weight, preferred_element_type=jnp.float32
    ).astype(jnp.bfloat16)
    query = projected[0].reshape(group_rows, span_count, head_count, HD)
    factor = 1.0 / HD**0.5
    running = jnp.full((head_count, span_count, group_rows), -1e30, jnp.float32)
    key_piece = lax.all_gather(projected[1], "span", axis=1, tiled=True)
    value_piece = lax.all_gather(projected[2], "span", axis=1, tiled=True)
    piece_spans = key_piece.shape[1]
    key_four = key_piece.reshape(group_rows, piece_spans, head_count, HD)
    value_four = value_piece.reshape(group_rows, piece_spans, head_count, HD)
    allowed = (span_order[None, :] <= my_places[:, None])[None, :, None, :, None]
    scores = (
        jnp.einsum("tahd,ubhd->hatbu", query, key_four, preferred_element_type=jnp.float32) * factor
    )
    scores = jnp.where(allowed, scores, -1e30)
    newest = jnp.maximum(running, jnp.max(scores, axis=(3, 4)))
    expo = jnp.where(allowed, jnp.exp(scores - newest[..., None, None]), 0.0)
    denom = jnp.sum(expo, axis=(3, 4))
    accum = jnp.einsum(
        "hatbu,ubhd->hatd",
        expo.astype(jnp.bfloat16),
        value_four,
        preferred_element_type=jnp.float32,
    )
    running, denom, accum = (newest, denom, accum)
    attended = (
        (accum / denom[..., None])
        .transpose(2, 1, 0, 3)
        .reshape(group_rows, span_count, head_count * HD)
        .astype(jnp.bfloat16)
    )
    rows = attended
    attn_sum = lax.psum_scatter(
        jnp.einsum("tck,kd->tcd", rows, out_weight, preferred_element_type=jnp.float32).astype(
            jnp.bfloat16
        ),
        "space",
        scatter_dimension=0,
        tiled=True,
    ).astype(jnp.float32)
    residual = (latents.astype(jnp.float32) + modulation[None, :, 2] * attn_sum).astype(
        jnp.bfloat16
    )
    second = norm_mod(
        lax.all_gather(residual, "space", axis=0, tiled=True).astype(jnp.float32),
        modulation[None, :, 3],
        modulation[None, :, 4],
    )
    hidden = jax.nn.gelu(
        jnp.einsum("tcd,df->tcf", second, up_weight, preferred_element_type=jnp.float32),
        approximate=True,
    ).astype(jnp.bfloat16)
    rows = hidden
    ffn_sum = lax.psum_scatter(
        jnp.einsum("tcf,fd->tcd", rows, down_weight, preferred_element_type=jnp.float32).astype(
            jnp.bfloat16
        ),
        "space",
        scatter_dimension=0,
        tiled=True,
    ).astype(jnp.float32)
    return (residual.astype(jnp.float32) + modulation[None, :, 5] * ffn_sum).astype(jnp.bfloat16)


def flip(index, bit):
    return index + bit * (1 - 2 * ((index // bit) % 2))


def layer_kernel(
    nz, ns, span_count, order_ref, key_span_ref, latent_ref, mod_ref, qkv_hbm, out_hbm, up_hbm, down_hbm,
    mixed_ref,
    x_ref, w_a, w_b, w_out, w_up, gathered, normed, query, kv, expo, scores, denom, attended, part,
    from_left, from_right, from_left2, from_right2, resid, hidden, acc, key_order_ref,
    w_sem, ag_send, ag_recv, kv_send, kv_recv, rs_send, rs_recv,
):
    z = lax.axis_index("space")
    me = lax.axis_index("span")
    rows, width = x_ref.shape
    tok = rows // span_count
    wide = width // CHUNKS
    last = nz - 1
    heads = query.shape[2] // HD
    down_blocks = width // BLOCK
    first_blocks = w_b.shape[0]

    def load(src, dst, slot):
        return pltpu.make_async_copy(src, dst, w_sem.at[slot])

    def columns(c, size):
        return pl.ds(c * size, size)

    qkv_loads = [load(qkv_hbm.at[i], w_a.at[i], i) for i in range(3)]
    out_load = load(out_hbm, w_out, 3)
    up_loads = [load(up_hbm.at[:, columns(i, BLOCK)], w_up.at[i], 4 + i) for i in range(w_up.shape[0])]
    down_base = 4 + w_up.shape[0]
    down_loads = [
        load(
            down_hbm.at[:, columns(i, BLOCK)],
            w_b.at[i] if i < first_blocks else w_a.at[i - first_blocks],
            down_base + i,
        )
        for i in range(down_blocks)
    ]
    for i in (1, 2, 0):
        qkv_loads[i].start()
    stored = latent_ref[...].astype(jnp.float32)
    x_ref[...] = jnp.concatenate([stored[:, a, :] for a in range(span_count)], axis=0).astype(jnp.bfloat16)

    barrier = pltpu.get_barrier_semaphore()
    for bit in (1, 2, 4):
        pl.semaphore_signal(barrier, inc=1, device_id=(flip(me, bit), z), device_id_type=MESH)

    @pl.when(z > 0)
    def _():
        pl.semaphore_signal(barrier, inc=1, device_id=(me, z - 1), device_id_type=MESH)

    @pl.when(z < last)
    def _():
        pl.semaphore_signal(barrier, inc=1, device_id=(me, z + 1), device_id_type=MESH)

    pl.semaphore_wait(barrier, 3 + jnp.where(z > 0, 1, 0) + jnp.where(z < last, 1, 0))

    def ag_copy(which, way, s, c, src, dst):
        return pltpu.make_async_remote_copy(
            src_ref=src, dst_ref=dst,
            send_sem=ag_send.at[which, way, s, c], recv_sem=ag_recv.at[which, way, s, c],
            device_id=(me, z + 1 if way == 0 else z - 1), device_id_type=MESH,
        )

    def ag_sends(way, s):
        return jnp.logical_and(z < last, z - s >= 0) if way == 0 else jnp.logical_and(z > 0, z + s <= last)

    def ag_gets(way, s):
        return z - 1 - s >= 0 if way == 0 else z + 1 + s <= last

    def ag_own(which, own, buf, c):
        for way in range(2):
            @pl.when(ag_sends(way, 0))
            def _():
                ag_copy(which, way, 0, c, own.at[:, columns(c, wide)], buf.at[z, :, columns(c, wide)]).start()

    def ag_step(which, buf, s, c):
        for way in range(2):
            block = z - 1 - s if way == 0 else z + 1 + s

            @pl.when(ag_gets(way, s))
            def _():
                piece = buf.at[block, :, columns(c, wide)]
                ag_copy(which, way, s, c, piece, piece).wait_recv()

            if s + 1 < last:
                @pl.when(ag_sends(way, s + 1))
                def _():
                    piece = buf.at[block, :, columns(c, wide)]
                    ag_copy(which, way, s + 1, c, piece, piece).start()

    def ag_drain(which, buf):
        for way in range(2):
            for s in range(last):
                for c in range(CHUNKS):
                    @pl.when(ag_sends(way, s))
                    def _():
                        piece = buf.at[0, :, columns(c, wide)]
                        ag_copy(which, way, s, c, piece, piece).wait_send()

    def norm_block(block, first):
        r = block.astype(jnp.float32)
        centred = r - jnp.mean(r, axis=-1, keepdims=True)
        variance = jnp.mean(centred * centred, axis=-1, keepdims=True)
        y = centred * lax.rsqrt(variance + 1e-06)
        pieces = []
        for a in range(span_count):
            shift = mod_ref[first, a : a + 1, :]
            scale = mod_ref[first + 1, a : a + 1, :]
            pieces.append(y[a * tok : (a + 1) * tok] * (1.0 + scale) + shift)
        return jnp.concatenate(pieces, axis=0).astype(jnp.bfloat16)

    def flip_all(index, rel):
        for bit in (1, 2, 4):
            if rel & bit:
                index = flip(index, bit)
        return index

    def kv_copy(which, rel, bit, block):
        piece = kv.at[which, flip_all(me, rel ^ bit), block]
        return pltpu.make_async_remote_copy(
            src_ref=piece, dst_ref=piece,
            send_sem=kv_send.at[which, rel, block], recv_sem=kv_recv.at[which, rel, block],
            device_id=(flip(me, bit), z), device_id_type=MESH,
        )

    def kv_take(which, rel, block):
        piece = kv.at[which, flip_all(me, rel), block]
        pltpu.make_async_remote_copy(
            src_ref=piece, dst_ref=piece,
            send_sem=kv_send.at[which, rel, block], recv_sem=kv_recv.at[which, rel, block],
            device_id=(flip(me, 1), z), device_id_type=MESH,
        ).wait_recv()

    def project(block, source, first):
        rows_in = norm_block(source, 0)

        def part_of(i):
            if first:
                qkv_loads[i].wait()
            return jnp.dot(rows_in, w_a[i], preferred_element_type=jnp.float32).astype(jnp.bfloat16)

        for which in range(2):
            kv[which, me, block] = part_of(1 + which)
            for bit in ((2, 4, 1), (4, 2, 1))[which]:
                kv_copy(which, bit, bit, block).start()
        query[block] = part_of(0)

    def second_hop(block):
        kv_take(0, 2, block)
        kv_copy(0, 6, 4, block).start()
        kv_copy(0, 3, 1, block).start()
        kv_take(1, 4, block)
        kv_copy(1, 6, 2, block).start()
        kv_copy(1, 5, 1, block).start()
        kv_take(0, 4, block)
        kv_copy(0, 5, 1, block).start()
        kv_take(1, 2, block)
        kv_copy(1, 3, 1, block).start()

    def third_hop(block):
        for which in range(2):
            kv_take(which, 6, block)
            kv_copy(which, 7, 1, block).start()

    def each_block(s, do):
        if s == -1:
            do(z)
        elif s >= 0:
            for way in range(2):
                @pl.when(ag_gets(way, s))
                def _():
                    do(z - 1 - s if way == 0 else z + 1 + s)

    for c in range(CHUNKS):
        ag_own(0, x_ref, gathered, c)
    out_load.start()
    for copy in up_loads:
        copy.start()
    for copy in down_loads[:first_blocks]:
        copy.start()
    project(z, x_ref[...], True)
    for s in range(last):
        for c in range(CHUNKS):
            ag_step(0, gathered, s, c)
        each_block(s, lambda block: project(block, gathered[block], False))
        each_block(s - 1, second_hop)
        each_block(s - 2, third_hop)
    for copy in down_loads[first_blocks:]:
        copy.start()
    each_block(last - 1, second_hop)
    each_block(last - 2, third_hop)
    each_block(last - 1, third_hop)
    ag_drain(0, gathered)

    @pl.loop(0, nz)
    def _(block):
        for which in range(2):
            for rel in (1, 3, 5, 7):
                kv_take(which, rel, block)

    total_rows = nz * rows
    keys_rows = ns * total_rows
    factor = 1.0 / HD**0.5
    places = [order_ref[me * span_count + a] for a in range(span_count)]

    key_order = jnp.zeros((1, keys_rows), jnp.int32)
    for span in range(ns * span_count):
        key_order = jnp.where(key_span_ref[...] == span, order_ref[span], key_order)
    key_order_ref[...] = key_order

    def head_scores(h):
        key_order = key_order_ref[...]
        lanes = pl.ds(pl.multiple_of(h * HD, HD), HD)
        keys = kv[0, :, :, :, lanes].reshape(keys_rows, HD)
        scores[...] = lax.dot_general(
            query[:, :, lanes].reshape(total_rows, HD), keys, (((1,), (1,)), ((), ())), preferred_element_type=jnp.float32
        )
        for block in range(nz):
            out = []
            sums = []
            for a in range(span_count):
                at = block * rows + a * tok
                allowed = key_order <= places[a]
                sc = jnp.where(allowed, scores[at : at + tok, :] * factor, -1e30)
                e = jnp.exp(sc - jnp.max(sc, axis=-1, keepdims=True))
                e = jnp.where(allowed, e, 0.0)
                out.append(e)
                sums.append(jnp.broadcast_to(jnp.sum(e, axis=-1, keepdims=True), (tok, HD)))
            expo[h, block * rows : (block + 1) * rows, :] = jnp.concatenate(out, axis=0).astype(jnp.bfloat16)
            denom[h, block * rows : (block + 1) * rows, :] = jnp.concatenate(sums, axis=0)

    @pl.loop(0, heads)
    def _(h):
        head_scores(h)

    @pl.loop(0, heads)
    def _(h):
        lanes = pl.ds(pl.multiple_of(h * HD, HD), HD)
        mixed_values = jnp.dot(
            expo[h], kv[1, :, :, :, lanes].reshape(keys_rows, HD), preferred_element_type=jnp.float32
        )
        attended[:, lanes] = (mixed_values / denom[h]).astype(jnp.bfloat16)

    @pl.loop(0, nz)
    def _(block):
        for which in range(2):
            for rel in range(1, 8):
                bit = rel & -rel if rel != 6 else (4 if which == 0 else 2)
                kv_copy(which, rel, bit, block).wait_send()

    def rs_copy(which, way, s, c, owner):
        buf = ((from_left, from_right), (from_left2, from_right2))[which][way]
        return pltpu.make_async_remote_copy(
            src_ref=part.at[owner, :, columns(c, wide)], dst_ref=buf.at[owner, :, columns(c, wide)],
            send_sem=rs_send.at[which, way, s, c], recv_sem=rs_recv.at[which, way, s, c],
            device_id=(me, z + 1 if way == 0 else z - 1), device_id_type=MESH,
        )

    def rs_start(which, c):
        @pl.when(z == 0)
        def _():
            for s in range(last):
                rs_copy(which, 0, s, c, last - s).start()

        @pl.when(z == last)
        def _():
            for s in range(last):
                rs_copy(which, 1, s, c, s).start()

    def rs_pass(which, c):
        for s in range(last):
            for way in range(2):
                owner = last - s if way == 0 else s
                on = jnp.logical_and(z > 0, owner > z) if way == 0 else jnp.logical_and(z < last, owner < z)

                @pl.when(on)
                def _():
                    copy = rs_copy(which, way, s, c, owner)
                    copy.wait_recv()
                    buf = ((from_left, from_right), (from_left2, from_right2))[which][way]
                    at = columns(c, wide)
                    part[owner, :, at] = (
                        part[owner, :, at].astype(jnp.float32) + buf[owner, :, at].astype(jnp.float32)
                    ).astype(jnp.bfloat16)
                    copy.start()

        acc[...] = part[z, :, columns(c, wide)].astype(jnp.float32)

        @pl.when(z > 0)
        def _():
            rs_copy(which, 0, last - z, c, z).wait_recv()
            buf = (from_left, from_left2)[which]
            acc[...] += buf[z, :, columns(c, wide)].astype(jnp.float32)

        @pl.when(z < last)
        def _():
            rs_copy(which, 1, z, c, z).wait_recv()
            buf = (from_right, from_right2)[which]
            acc[...] += buf[z, :, columns(c, wide)].astype(jnp.float32)

    def rs_drain(which):
        for s in range(last):
            for way in range(2):
                owner = last - s if way == 0 else s
                for c in range(CHUNKS):
                    @pl.when(owner > z if way == 0 else owner < z)
                    def _():
                        rs_copy(which, way, s, c, owner).wait_send()

    def gated(base, gate, c):
        pieces = []
        for a in range(span_count):
            span_rows = slice(a * tok, (a + 1) * tok)
            factor_row = mod_ref[gate, a : a + 1, columns(c, wide)]
            pieces.append(base[span_rows] + factor_row * acc[span_rows, :])
        return jnp.concatenate(pieces, axis=0).astype(jnp.bfloat16)

    out_load.wait()
    for c in range(CHUNKS):
        part[:, :, columns(c, wide)] = (
            jnp.dot(attended[...], w_out[:, columns(c, wide)], preferred_element_type=jnp.float32)
            .astype(jnp.bfloat16)
            .reshape(nz, rows, wide)
        )
        rs_start(0, c)
    for c in range(CHUNKS + last - 1):
        if c < CHUNKS:
            at = columns(c, wide)
            rs_pass(0, c)
            resid[z, :, at] = gated(x_ref[:, at].astype(jnp.float32), 2, c)
            ag_own(1, resid.at[z], resid, c)
        for s in range(last - 1):
            if 0 <= c - 1 - s < CHUNKS:
                ag_step(1, resid, s, c - 1 - s)
    rs_drain(0)
    for c in range(CHUNKS):
        ag_step(1, resid, last - 1, c)

    @pl.loop(0, nz)
    def _(block):
        normed[block] = norm_block(resid[block], 3)

    for copy in up_loads:
        copy.wait()

    @pl.loop(0, w_up.shape[0])
    def _(i):
        raised = jnp.dot(
            normed[...].reshape(total_rows, width), w_up[i], preferred_element_type=jnp.float32
        )
        hidden[:, pl.ds(pl.multiple_of(i * BLOCK, BLOCK), BLOCK)] = jax.nn.gelu(
            raised, approximate=True
        ).astype(jnp.bfloat16)

    ag_drain(1, resid)
    done = 0
    for i in range(down_blocks):
        down_loads[i].wait()
        weight = w_b[i] if i < first_blocks else w_a[i - first_blocks]
        part[:, :, columns(i, BLOCK)] = (
            jnp.dot(hidden[...], weight, preferred_element_type=jnp.float32)
            .astype(jnp.bfloat16)
            .reshape(nz, rows, BLOCK)
        )
        while done < CHUNKS and (done + 1) * wide <= (i + 1) * BLOCK:
            rs_start(1, done)
            done += 1
    for c in range(CHUNKS):
        at = columns(c, wide)
        rs_pass(1, c)
        mixed_ref[:, at] = gated(resid[z, :, at].astype(jnp.float32), 5, c)
    rs_drain(1)


def kernel_body(nz, ns, latents, span_order, modulation, qkv_weight, out_weight, up_weight, down_weight):
    tok, span_count, width = latents.shape
    rows = tok * span_count
    total = rows * nz
    head_cols = qkv_weight.shape[2]
    heads = head_cols // HD
    hid = up_weight.shape[1]
    keys_rows = ns * total
    key_span = np.broadcast_to(
        np.arange(ns * span_count, dtype=np.int32).reshape(ns, 1, span_count, 1), (ns, nz, span_count, tok)
    ).reshape(1, keys_rows)
    blocks = width // BLOCK
    later = qkv_weight.shape[0]
    bf, f32 = jnp.bfloat16, jnp.float32
    vmem = pl.BlockSpec(memory_space=pltpu.VMEM)
    hbm = pl.BlockSpec(memory_space=pl.ANY)
    grouped = pltpu.VMEM((nz, rows, width), bf)
    flops = 2 * total * width * (4 * head_cols + 2 * hid) + 4 * total * keys_rows * head_cols
    mixed = pl.pallas_call(
        functools.partial(layer_kernel, nz, ns, span_count),
        out_shape=jax.ShapeDtypeStruct((rows, width), bf),
        in_specs=[pl.BlockSpec(memory_space=pltpu.SMEM), vmem, vmem, vmem, hbm, hbm, hbm, hbm],
        out_specs=vmem,
        scratch_shapes=[
            pltpu.VMEM((rows, width), bf),
            pltpu.VMEM((later, width, head_cols), bf),
            pltpu.VMEM((blocks - later, hid, BLOCK), bf),
            pltpu.VMEM((head_cols, width), bf),
            pltpu.VMEM((hid // BLOCK, width, BLOCK), bf),
            grouped,
            grouped,
            pltpu.VMEM((nz, rows, head_cols), bf),
            pltpu.VMEM((2, ns, nz, rows, head_cols), bf),
            pltpu.VMEM((heads, total, keys_rows), bf),
            pltpu.VMEM((total, keys_rows), f32),
            pltpu.VMEM((heads, total, HD), f32),
            pltpu.VMEM((total, head_cols), bf),
            grouped,
            grouped,
            grouped,
            grouped,
            grouped,
            grouped,
            pltpu.VMEM((total, hid), bf),
            pltpu.VMEM((rows, width // CHUNKS), f32),
            pltpu.VMEM((1, keys_rows), jnp.int32),
            pltpu.SemaphoreType.DMA((4 + hid // BLOCK + blocks,)),
            pltpu.SemaphoreType.DMA((2, 2, nz - 1, CHUNKS)),
            pltpu.SemaphoreType.DMA((2, 2, nz - 1, CHUNKS)),
            pltpu.SemaphoreType.DMA((2, ns, nz)),
            pltpu.SemaphoreType.DMA((2, ns, nz)),
            pltpu.SemaphoreType.DMA((2, 2, nz - 1, CHUNKS)),
            pltpu.SemaphoreType.DMA((2, 2, nz - 1, CHUNKS)),
        ],
        compiler_params=pltpu.CompilerParams(
            collective_id=0, has_side_effects=True, vmem_limit_bytes=VMEM_BYTES
        ),
        cost_estimate=pl.CostEstimate(
            flops=flops,
            bytes_accessed=2 * width * (4 * head_cols + 2 * hid),
            transcendentals=total * (keys_rows * heads + hid),
        ),
    )(span_order, key_span, latents, modulation.transpose(1, 0, 2), qkv_weight, out_weight, up_weight, down_weight)
    return mixed.reshape(span_count, tok, width).transpose(1, 0, 2)


def fits(nz, ns, tok, span_count, width, head_cols, hid):
    rows = tok * span_count
    total = rows * nz
    keys_rows = ns * total
    weights = 2 * width * (4 * head_cols + 2 * hid) - 2 * width * 3 * head_cols
    moving = 2 * (9 * total * width + 2 * (keys_rows + total) * head_cols)
    moving += 2 * total * keys_rows * (head_cols // HD + 2) + 4 * total * head_cols
    return (
        ns == 8
        and nz > 1
        and rows % 16 == 0
        and tok % 8 == 0
        and head_cols == BLOCK
        and width == hid
        and width % BLOCK == 0
        and width % (CHUNKS * HD) == 0
        and weights + moving < VMEM_BYTES
    )


def body(nz, ns, latents, span_order, modulation, qkv_weight, out_weight, up_weight, down_weight):
    args = (latents, span_order, modulation, qkv_weight, out_weight, up_weight, down_weight)
    if fits(nz, ns, *latents.shape, qkv_weight.shape[2], up_weight.shape[1]):
        return kernel_body(nz, ns, *args)
    return plain_body(*args)


def solution(mesh):
    return jax.shard_map(
        functools.partial(body, mesh.shape["space"], mesh.shape["span"]),
        mesh=mesh,
        in_specs=(
            P("space", "span", None),
            P(),
            P("span", None, None),
            P(None, None, "space"),
            P("space", None),
            P(None, "space"),
            P("space", None),
        ),
        out_specs=P("space", "span", None),
        check_vma=False,
    )
```

```python
import functools

import jax
import jax.numpy as jnp
import numpy as np
from jax import lax
from jax.experimental import pallas as pl
from jax.experimental.pallas import tpu as pltpu
from jax.sharding import PartitionSpec as P

HD = 128
CHUNKS = 6
BLOCK = 512
MESH = pl.DeviceIdType.MESH
VMEM_BYTES = 62 * 1024 * 1024


def norm_mod(rows, shift, scale):
    mean = jnp.mean(rows, axis=-1, keepdims=True)
    centred = rows - mean
    variance = jnp.mean(centred * centred, axis=-1, keepdims=True)
    return (centred * lax.rsqrt(variance + 1e-06) * (1.0 + scale) + shift).astype(jnp.bfloat16)


def plain_body(latents, span_order, modulation, qkv_weight, out_weight, up_weight, down_weight):
    span_count = latents.shape[1]
    head_count = qkv_weight.shape[2] // HD
    my_start = lax.axis_index("span") * span_count
    my_places = lax.dynamic_slice_in_dim(span_order, my_start, span_count, 0)
    gathered = lax.all_gather(latents, "space", axis=0, tiled=True)
    group_rows = gathered.shape[0]
    gathered_f = gathered.astype(jnp.float32)
    normed = norm_mod(gathered_f, modulation[None, :, 0], modulation[None, :, 1])
    projected = jnp.einsum(
        "tcd,sdf->stcf", normed, qkv_weight, preferred_element_type=jnp.float32
    ).astype(jnp.bfloat16)
    query = projected[0].reshape(group_rows, span_count, head_count, HD)
    factor = 1.0 / HD**0.5
    running = jnp.full((head_count, span_count, group_rows), -1e30, jnp.float32)
    key_piece = lax.all_gather(projected[1], "span", axis=1, tiled=True)
    value_piece = lax.all_gather(projected[2], "span", axis=1, tiled=True)
    piece_spans = key_piece.shape[1]
    key_four = key_piece.reshape(group_rows, piece_spans, head_count, HD)
    value_four = value_piece.reshape(group_rows, piece_spans, head_count, HD)
    allowed = (span_order[None, :] <= my_places[:, None])[None, :, None, :, None]
    scores = (
        jnp.einsum("tahd,ubhd->hatbu", query, key_four, preferred_element_type=jnp.float32) * factor
    )
    scores = jnp.where(allowed, scores, -1e30)
    newest = jnp.maximum(running, jnp.max(scores, axis=(3, 4)))
    expo = jnp.where(allowed, jnp.exp(scores - newest[..., None, None]), 0.0)
    denom = jnp.sum(expo, axis=(3, 4))
    accum = jnp.einsum(
        "hatbu,ubhd->hatd",
        expo.astype(jnp.bfloat16),
        value_four,
        preferred_element_type=jnp.float32,
    )
    running, denom, accum = (newest, denom, accum)
    attended = (
        (accum / denom[..., None])
        .transpose(2, 1, 0, 3)
        .reshape(group_rows, span_count, head_count * HD)
        .astype(jnp.bfloat16)
    )
    rows = attended
    attn_sum = lax.psum_scatter(
        jnp.einsum("tck,kd->tcd", rows, out_weight, preferred_element_type=jnp.float32).astype(
            jnp.bfloat16
        ),
        "space",
        scatter_dimension=0,
        tiled=True,
    ).astype(jnp.float32)
    residual = (latents.astype(jnp.float32) + modulation[None, :, 2] * attn_sum).astype(
        jnp.bfloat16
    )
    second = norm_mod(
        lax.all_gather(residual, "space", axis=0, tiled=True).astype(jnp.float32),
        modulation[None, :, 3],
        modulation[None, :, 4],
    )
    hidden = jax.nn.gelu(
        jnp.einsum("tcd,df->tcf", second, up_weight, preferred_element_type=jnp.float32),
        approximate=True,
    ).astype(jnp.bfloat16)
    rows = hidden
    ffn_sum = lax.psum_scatter(
        jnp.einsum("tcf,fd->tcd", rows, down_weight, preferred_element_type=jnp.float32).astype(
            jnp.bfloat16
        ),
        "space",
        scatter_dimension=0,
        tiled=True,
    ).astype(jnp.float32)
    return (residual.astype(jnp.float32) + modulation[None, :, 5] * ffn_sum).astype(jnp.bfloat16)


def flip(index, bit):
    return index + bit * (1 - 2 * ((index // bit) % 2))


def layer_kernel(
    nz, ns, span_count, order_ref, key_span_ref, latent_ref, mod_ref, qkv_hbm, out_hbm, up_hbm, down_hbm,
    mixed_ref,
    x_ref, w_a, w_b, w_out, w_up, gathered, normed, query, kv, expo, scores, denom, attended, part,
    from_left, from_right, from_left2, from_right2, resid, hidden, acc, key_order_ref,
    w_sem, ag_send, ag_recv, kv_send, kv_recv, rs_send, rs_recv,
):
    z = lax.axis_index("space")
    me = lax.axis_index("span")
    rows, width = x_ref.shape
    whole = pl.ds(0, rows)
    cut = 16 * (rows // 16 - rows // 48)
    parts = (pl.ds(0, cut), pl.ds(cut, rows - cut))
    tok = rows // span_count
    wide = width // CHUNKS
    last = nz - 1
    heads = query.shape[2] // HD
    down_blocks = width // BLOCK
    first_blocks = w_b.shape[0]

    def load(src, dst, slot):
        return pltpu.make_async_copy(src, dst, w_sem.at[slot])

    def columns(c, size):
        return pl.ds(pl.multiple_of(c * size, size), size)

    qkv_loads = [load(qkv_hbm.at[i], w_a.at[i], i) for i in range(3)]
    out_load = load(out_hbm, w_out, 3)
    up_loads = [load(up_hbm.at[:, columns(i, BLOCK)], w_up.at[i], 4 + i) for i in range(w_up.shape[0])]
    down_base = 4 + w_up.shape[0]
    down_loads = [
        load(
            down_hbm.at[:, columns(i, BLOCK)],
            w_b.at[i] if i < first_blocks else w_a.at[i - first_blocks],
            down_base + i,
        )
        for i in range(down_blocks)
    ]
    for i in (1, 2, 0):
        qkv_loads[i].start()
    stored = latent_ref[...].astype(jnp.float32)
    x_ref[...] = jnp.concatenate([stored[:, a, :] for a in range(span_count)], axis=0).astype(jnp.bfloat16)

    barrier = pltpu.get_barrier_semaphore()
    for bit in (1, 2, 4):
        pl.semaphore_signal(barrier, inc=1, device_id=(flip(me, bit), z), device_id_type=MESH)

    @pl.when(z > 0)
    def _():
        pl.semaphore_signal(barrier, inc=1, device_id=(me, z - 1), device_id_type=MESH)

    @pl.when(z < last)
    def _():
        pl.semaphore_signal(barrier, inc=1, device_id=(me, z + 1), device_id_type=MESH)

    pl.semaphore_wait(barrier, 3 + jnp.where(z > 0, 1, 0) + jnp.where(z < last, 1, 0))

    def ag_copy(which, way, s, c, src, dst):
        return pltpu.make_async_remote_copy(
            src_ref=src, dst_ref=dst,
            send_sem=ag_send.at[which, way, s, c], recv_sem=ag_recv.at[which, way, s, c],
            device_id=(me, z + 1 if way == 0 else z - 1), device_id_type=MESH,
        )

    def ag_sends(way, s):
        return jnp.logical_and(z < last, z - s >= 0) if way == 0 else jnp.logical_and(z > 0, z + s <= last)

    def ag_gets(way, s):
        return z - 1 - s >= 0 if way == 0 else z + 1 + s <= last

    def ag_own(which, own, buf, c, at):
        for way in range(2):
            @pl.when(ag_sends(way, 0))
            def _():
                ag_copy(
                    which, way, 0, c, own.at[at, columns(c, wide)], buf.at[z, at, columns(c, wide)]
                ).start()

    def ag_step(which, buf, s, c, at):
        for way in range(2):
            block = z - 1 - s if way == 0 else z + 1 + s

            @pl.when(ag_gets(way, s))
            def _():
                piece = buf.at[block, at, columns(c, wide)]
                ag_copy(which, way, s, c, piece, piece).wait_recv()

            if s + 1 < last:
                @pl.when(ag_sends(way, s + 1))
                def _():
                    piece = buf.at[block, at, columns(c, wide)]
                    ag_copy(which, way, s + 1, c, piece, piece).start()

    def ag_drain(which, buf, at):
        @pl.loop(0, CHUNKS)
        def _(c):
            for way in range(2):
                for s in range(last):
                    @pl.when(ag_sends(way, s))
                    def _():
                        piece = buf.at[0, at, columns(c, wide)]
                        ag_copy(which, way, s, c, piece, piece).wait_send()

    def segments(at):
        first, end = at.start, at.start + at.size
        runs = []
        for a in range(span_count):
            low, high = max(first, a * tok), min(end, (a + 1) * tok)
            if low < high:
                runs.append((a, low - first, high - first))
        return runs

    def norm_block(block, first, at):
        r = block.astype(jnp.float32)
        centred = r - jnp.mean(r, axis=-1, keepdims=True)
        variance = jnp.mean(centred * centred, axis=-1, keepdims=True)
        y = centred * lax.rsqrt(variance + 1e-06)
        pieces = []
        for a, low, high in segments(at):
            shift = mod_ref[first, a : a + 1, :]
            scale = mod_ref[first + 1, a : a + 1, :]
            pieces.append(y[low:high] * (1.0 + scale) + shift)
        return jnp.concatenate(pieces, axis=0).astype(jnp.bfloat16)

    def flip_all(index, rel):
        for bit in (1, 2, 4):
            if rel & bit:
                index = flip(index, bit)
        return index

    def kv_copy(which, rel, bit, block):
        piece = kv.at[which, flip_all(me, rel ^ bit), block]
        return pltpu.make_async_remote_copy(
            src_ref=piece, dst_ref=piece,
            send_sem=kv_send.at[which, rel, block], recv_sem=kv_recv.at[which, rel, block],
            device_id=(flip(me, bit), z), device_id_type=MESH,
        )

    def kv_take(which, rel, block):
        piece = kv.at[which, flip_all(me, rel), block]
        pltpu.make_async_remote_copy(
            src_ref=piece, dst_ref=piece,
            send_sem=kv_send.at[which, rel, block], recv_sem=kv_recv.at[which, rel, block],
            device_id=(flip(me, 1), z), device_id_type=MESH,
        ).wait_recv()

    def project(block, source, first):
        rows_in = norm_block(source, 0, whole)

        def part_of(i):
            if first:
                qkv_loads[i].wait()
            return jnp.dot(rows_in, w_a[i], preferred_element_type=jnp.float32).astype(jnp.bfloat16)

        for which in range(2):
            kv[which, me, block] = part_of(1 + which)
            for bit in ((2, 4, 1), (4, 2, 1))[which]:
                kv_copy(which, bit, bit, block).start()
        query[block] = part_of(0)

    def second_hop(block):
        kv_take(0, 2, block)
        kv_copy(0, 6, 4, block).start()
        kv_copy(0, 3, 1, block).start()
        kv_take(1, 4, block)
        kv_copy(1, 6, 2, block).start()
        kv_copy(1, 5, 1, block).start()
        kv_take(0, 4, block)
        kv_copy(0, 5, 1, block).start()
        kv_take(1, 2, block)
        kv_copy(1, 3, 1, block).start()

    def third_hop(block):
        for which in range(2):
            kv_take(which, 6, block)
            kv_copy(which, 7, 1, block).start()

    def each_block(s, do):
        if s == -1:
            do(z)
        elif s >= 0:
            for way in range(2):
                @pl.when(ag_gets(way, s))
                def _():
                    do(z - 1 - s if way == 0 else z + 1 + s)

    @pl.loop(0, CHUNKS)
    def _(c):
        ag_own(0, x_ref, gathered, c, whole)

    out_load.start()
    for copy in up_loads:
        copy.start()
    for copy in down_loads[:first_blocks]:
        copy.start()
    project(z, x_ref[...], True)
    for s in range(last):
        @pl.loop(0, CHUNKS)
        def _(c):
            ag_step(0, gathered, s, c, whole)

        each_block(s, lambda block: project(block, gathered[block], False))
        each_block(s - 1, second_hop)
        each_block(s - 2, third_hop)
    for copy in down_loads[first_blocks:]:
        copy.start()
    each_block(last - 1, second_hop)
    each_block(last - 2, third_hop)
    each_block(last - 1, third_hop)
    ag_drain(0, gathered, whole)

    @pl.loop(0, nz)
    def _(block):
        for which in range(2):
            for rel in (1, 3, 5, 7):
                kv_take(which, rel, block)

    total_rows = nz * rows
    keys_rows = ns * total_rows
    factor = 1.0 / HD**0.5
    places = [order_ref[me * span_count + a] for a in range(span_count)]

    key_order = jnp.zeros((1, keys_rows), jnp.int32)
    for span in range(ns * span_count):
        key_order = jnp.where(key_span_ref[...] == span, order_ref[span], key_order)
    key_order_ref[...] = key_order

    def head_scores(h):
        key_order = key_order_ref[...]
        lanes = pl.ds(pl.multiple_of(h * HD, HD), HD)
        keys = kv[0, :, :, :, lanes].reshape(keys_rows, HD)
        scores[...] = lax.dot_general(
            query[:, :, lanes].reshape(total_rows, HD), keys, (((1,), (1,)), ((), ())), preferred_element_type=jnp.float32
        )
        for block in range(nz):
            out = []
            sums = []
            for a in range(span_count):
                at = block * rows + a * tok
                allowed = key_order <= places[a]
                sc = jnp.where(allowed, scores[at : at + tok, :] * factor, -1e30)
                e = jnp.exp(sc - jnp.max(sc, axis=-1, keepdims=True))
                e = jnp.where(allowed, e, 0.0)
                out.append(e)
                sums.append(jnp.broadcast_to(jnp.sum(e, axis=-1, keepdims=True), (tok, HD)))
            expo[h, block * rows : (block + 1) * rows, :] = jnp.concatenate(out, axis=0).astype(jnp.bfloat16)
            denom[h, block * rows : (block + 1) * rows, :] = jnp.concatenate(sums, axis=0)

    @pl.loop(0, heads)
    def _(h):
        head_scores(h)

    @pl.loop(0, heads)
    def _(h):
        lanes = pl.ds(pl.multiple_of(h * HD, HD), HD)
        mixed_values = jnp.dot(
            expo[h], kv[1, :, :, :, lanes].reshape(keys_rows, HD), preferred_element_type=jnp.float32
        )
        attended[:, lanes] = (mixed_values / denom[h]).astype(jnp.bfloat16)

    @pl.loop(0, nz)
    def _(block):
        for which in range(2):
            for rel in range(1, 8):
                bit = rel & -rel if rel != 6 else (4 if which == 0 else 2)
                kv_copy(which, rel, bit, block).wait_send()

    def rs_buf(stage, way):
        return ((from_left, from_right), (from_left2, from_right2))[stage][way]

    def rs_copy(stage, p, way, s, c, owner):
        at = parts[p]
        return pltpu.make_async_remote_copy(
            src_ref=part.at[owner, at, columns(c, wide)],
            dst_ref=rs_buf(stage, way).at[owner, at, columns(c, wide)],
            send_sem=rs_send.at[2 * stage + p, way, s, c], recv_sem=rs_recv.at[2 * stage + p, way, s, c],
            device_id=(me, z + 1 if way == 0 else z - 1), device_id_type=MESH,
        )

    def rs_start(stage, p, c):
        @pl.when(z == 0)
        def _():
            for s in range(last):
                rs_copy(stage, p, 0, s, c, last - s).start()

        @pl.when(z == last)
        def _():
            for s in range(last):
                rs_copy(stage, p, 1, s, c, s).start()

    def rs_pass(stage, p, c):
        at, cols = parts[p], columns(c, wide)
        size = at.size
        for s in range(last):
            for way in range(2):
                owner = last - s if way == 0 else s
                on = jnp.logical_and(z > 0, owner > z) if way == 0 else jnp.logical_and(z < last, owner < z)

                @pl.when(on)
                def _():
                    copy = rs_copy(stage, p, way, s, c, owner)
                    copy.wait_recv()
                    part[owner, at, cols] = (
                        part[owner, at, cols].astype(jnp.float32)
                        + rs_buf(stage, way)[owner, at, cols].astype(jnp.float32)
                    ).astype(jnp.bfloat16)
                    copy.start()

        acc[0:size, :] = part[z, at, cols].astype(jnp.float32)

        @pl.when(z > 0)
        def _():
            rs_copy(stage, p, 0, last - z, c, z).wait_recv()
            acc[0:size, :] += rs_buf(stage, 0)[z, at, cols].astype(jnp.float32)

        @pl.when(z < last)
        def _():
            rs_copy(stage, p, 1, z, c, z).wait_recv()
            acc[0:size, :] += rs_buf(stage, 1)[z, at, cols].astype(jnp.float32)

    def rs_drain(stage, p):
        @pl.loop(0, CHUNKS)
        def _(c):
            for s in range(last):
                for way in range(2):
                    owner = last - s if way == 0 else s

                    @pl.when(owner > z if way == 0 else owner < z)
                    def _():
                        rs_copy(stage, p, way, s, c, owner).wait_send()

    def gated(base, gate, c, at):
        base = base.astype(jnp.float32)
        pieces = []
        for a, low, high in segments(at):
            row = mod_ref[gate, a : a + 1, columns(c, wide)]
            pieces.append(base[low:high] + row * acc[low:high, :])
        return jnp.concatenate(pieces, axis=0).astype(jnp.bfloat16)

    def residual_step(p, c):
        at, cols = parts[p], columns(c, wide)
        rs_pass(0, p, c)
        resid[z, at, cols] = gated(x_ref[at, cols], 2, c, at)
        ag_own(1 + p, resid.at[z], resid, c, at)
        for s in range(last - 1):
            @pl.when(c >= 1 + s)
            def _():
                ag_step(1 + p, resid, s, c - 1 - s, at)

    def residual_tail(p):
        at = parts[p]
        for c in range(CHUNKS, CHUNKS + last - 1):
            for s in range(last - 1):
                if 0 <= c - 1 - s < CHUNKS:
                    ag_step(1 + p, resid, s, c - 1 - s, at)

        @pl.loop(0, CHUNKS)
        def _(c):
            ag_step(1 + p, resid, last - 1, c, at)

    def second_norm(p):
        at = parts[p]

        @pl.loop(0, nz)
        def _(block):
            normed[block, at, :] = norm_block(resid[block, at, :], 3, at)

    def up(p, i):
        at = parts[p]
        raised = jnp.dot(
            normed[:, at, :].reshape(nz * at.size, width), w_up[i], preferred_element_type=jnp.float32
        )
        hidden[:, at, columns(i, BLOCK)] = (
            jax.nn.gelu(raised, approximate=True).astype(jnp.bfloat16).reshape(nz, at.size, BLOCK)
        )

    def down(p, i, weight):
        at = parts[p]
        part[:, at, columns(i, BLOCK)] = (
            jnp.dot(
                hidden[:, at, :].reshape(nz * at.size, hidden.shape[2]),
                weight,
                preferred_element_type=jnp.float32,
            )
            .astype(jnp.bfloat16)
            .reshape(nz, at.size, BLOCK)
        )
        rs_start(1, p, i)

    def finish(p, c):
        at, cols = parts[p], columns(c, wide)
        rs_pass(1, p, c)
        mixed_ref[at, cols] = gated(resid[z, at, cols], 5, c, at)

    out_load.wait()

    @pl.loop(0, CHUNKS)
    def _(c):
        part[:, :, columns(c, wide)] = (
            jnp.dot(attended[...], w_out[:, columns(c, wide)], preferred_element_type=jnp.float32)
            .astype(jnp.bfloat16)
            .reshape(nz, rows, wide)
        )
        rs_start(0, 0, c)

    @pl.loop(0, CHUNKS)
    def _(c):
        residual_step(0, c)
        rs_start(0, 1, c)

    residual_tail(0)
    second_norm(0)
    for copy in up_loads:
        copy.wait()

    @pl.loop(0, CHUNKS)
    def _(c):
        residual_step(1, c)
        up(0, c)

    for copy in down_loads:
        copy.wait()
    rs_drain(0, 0)
    rs_drain(0, 1)

    @pl.loop(0, first_blocks)
    def _(i):
        down(0, i, w_b[i])

    residual_tail(1)

    @pl.loop(first_blocks, down_blocks)
    def _(i):
        down(0, i, w_a[i - first_blocks])

    second_norm(1)
    early = CHUNKS // 2

    @pl.loop(0, early)
    def _(c):
        up(1, 2 * c)
        up(1, 2 * c + 1)
        finish(0, c)

    @pl.loop(0, early)
    def _(c):
        down(1, c, w_b[c])
        finish(0, early + c)

    @pl.loop(first_blocks, down_blocks)
    def _(i):
        down(1, i, w_a[i - first_blocks])

    @pl.loop(0, CHUNKS)
    def _(c):
        finish(1, c)

    for p in range(2):
        ag_drain(1 + p, resid, parts[p])
        rs_drain(1, p)


def kernel_body(nz, ns, latents, span_order, modulation, qkv_weight, out_weight, up_weight, down_weight):
    tok, span_count, width = latents.shape
    rows = tok * span_count
    total = rows * nz
    head_cols = qkv_weight.shape[2]
    heads = head_cols // HD
    hid = up_weight.shape[1]
    keys_rows = ns * total
    key_span = np.broadcast_to(
        np.arange(ns * span_count, dtype=np.int32).reshape(ns, 1, span_count, 1), (ns, nz, span_count, tok)
    ).reshape(1, keys_rows)
    blocks = width // BLOCK
    later = qkv_weight.shape[0]
    bf, f32 = jnp.bfloat16, jnp.float32
    vmem = pl.BlockSpec(memory_space=pltpu.VMEM)
    hbm = pl.BlockSpec(memory_space=pl.ANY)
    grouped = pltpu.VMEM((nz, rows, width), bf)
    flops = 2 * total * width * (4 * head_cols + 2 * hid) + 4 * total * keys_rows * head_cols
    mixed = pl.pallas_call(
        functools.partial(layer_kernel, nz, ns, span_count),
        out_shape=jax.ShapeDtypeStruct((rows, width), bf),
        in_specs=[pl.BlockSpec(memory_space=pltpu.SMEM), vmem, vmem, vmem, hbm, hbm, hbm, hbm],
        out_specs=vmem,
        scratch_shapes=[
            pltpu.VMEM((rows, width), bf),
            pltpu.VMEM((later, width, head_cols), bf),
            pltpu.VMEM((blocks - later, hid, BLOCK), bf),
            pltpu.VMEM((head_cols, width), bf),
            pltpu.VMEM((hid // BLOCK, width, BLOCK), bf),
            grouped,
            grouped,
            pltpu.VMEM((nz, rows, head_cols), bf),
            pltpu.VMEM((2, ns, nz, rows, head_cols), bf),
            pltpu.VMEM((heads, total, keys_rows), bf),
            pltpu.VMEM((total, keys_rows), f32),
            pltpu.VMEM((heads, total, HD), f32),
            pltpu.VMEM((total, head_cols), bf),
            grouped,
            grouped,
            grouped,
            grouped,
            grouped,
            grouped,
            pltpu.VMEM((nz, rows, hid), bf),
            pltpu.VMEM((rows, width // CHUNKS), f32),
            pltpu.VMEM((1, keys_rows), jnp.int32),
            pltpu.SemaphoreType.DMA((4 + hid // BLOCK + blocks,)),
            pltpu.SemaphoreType.DMA((3, 2, nz - 1, CHUNKS)),
            pltpu.SemaphoreType.DMA((3, 2, nz - 1, CHUNKS)),
            pltpu.SemaphoreType.DMA((2, ns, nz)),
            pltpu.SemaphoreType.DMA((2, ns, nz)),
            pltpu.SemaphoreType.DMA((4, 2, nz - 1, CHUNKS)),
            pltpu.SemaphoreType.DMA((4, 2, nz - 1, CHUNKS)),
        ],
        compiler_params=pltpu.CompilerParams(
            collective_id=0, has_side_effects=True, vmem_limit_bytes=VMEM_BYTES
        ),
        cost_estimate=pl.CostEstimate(
            flops=flops,
            bytes_accessed=2 * width * (4 * head_cols + 2 * hid),
            transcendentals=total * (keys_rows * heads + hid),
        ),
    )(span_order, key_span, latents, modulation.transpose(1, 0, 2), qkv_weight, out_weight, up_weight, down_weight)
    return mixed.reshape(span_count, tok, width).transpose(1, 0, 2)


def fits(nz, ns, tok, span_count, width, head_cols, hid):
    rows = tok * span_count
    total = rows * nz
    keys_rows = ns * total
    weights = 2 * width * (4 * head_cols + 2 * hid) - 2 * width * 3 * head_cols
    moving = 2 * (9 * total * width + 2 * (keys_rows + total) * head_cols)
    moving += 2 * total * keys_rows * (head_cols // HD + 2) + 4 * total * head_cols
    return (
        ns == 8
        and nz > 1
        and rows % 48 == 0
        and tok % 8 == 0
        and head_cols == BLOCK
        and width == hid
        and width == CHUNKS * BLOCK
        and weights + moving < VMEM_BYTES
    )


def body(nz, ns, latents, span_order, modulation, qkv_weight, out_weight, up_weight, down_weight):
    args = (latents, span_order, modulation, qkv_weight, out_weight, up_weight, down_weight)
    if fits(nz, ns, *latents.shape, qkv_weight.shape[2], up_weight.shape[1]):
        return kernel_body(nz, ns, *args)
    return plain_body(*args)


def solution(mesh):
    return jax.shard_map(
        functools.partial(body, mesh.shape["space"], mesh.shape["span"]),
        mesh=mesh,
        in_specs=(
            P("space", "span", None),
            P(),
            P("span", None, None),
            P(None, None, "space"),
            P("space", None),
            P(None, "space"),
            P("space", None),
        ),
        out_specs=P("space", "span", None),
        check_vma=False,
    )
```

```python
import functools

import jax
import jax.numpy as jnp
import numpy as np
from jax import lax
from jax.experimental import pallas as pl
from jax.experimental.pallas import tpu as pltpu
from jax.sharding import PartitionSpec as P

HD = 128
CHUNKS = 6
BLOCK = 512
MESH = pl.DeviceIdType.MESH
VMEM_BYTES = 62 * 1024 * 1024


def norm_mod(rows, shift, scale):
    mean = jnp.mean(rows, axis=-1, keepdims=True)
    centred = rows - mean
    variance = jnp.mean(centred * centred, axis=-1, keepdims=True)
    return (centred * lax.rsqrt(variance + 1e-06) * (1.0 + scale) + shift).astype(jnp.bfloat16)


def plain_body(latents, span_order, modulation, qkv_weight, out_weight, up_weight, down_weight):
    span_count = latents.shape[1]
    head_count = qkv_weight.shape[2] // HD
    my_start = lax.axis_index("span") * span_count
    my_places = lax.dynamic_slice_in_dim(span_order, my_start, span_count, 0)
    gathered = lax.all_gather(latents, "space", axis=0, tiled=True)
    group_rows = gathered.shape[0]
    gathered_f = gathered.astype(jnp.float32)
    normed = norm_mod(gathered_f, modulation[None, :, 0], modulation[None, :, 1])
    projected = jnp.einsum(
        "tcd,sdf->stcf", normed, qkv_weight, preferred_element_type=jnp.float32
    ).astype(jnp.bfloat16)
    query = projected[0].reshape(group_rows, span_count, head_count, HD)
    factor = 1.0 / HD**0.5
    running = jnp.full((head_count, span_count, group_rows), -1e30, jnp.float32)
    key_piece = lax.all_gather(projected[1], "span", axis=1, tiled=True)
    value_piece = lax.all_gather(projected[2], "span", axis=1, tiled=True)
    piece_spans = key_piece.shape[1]
    key_four = key_piece.reshape(group_rows, piece_spans, head_count, HD)
    value_four = value_piece.reshape(group_rows, piece_spans, head_count, HD)
    allowed = (span_order[None, :] <= my_places[:, None])[None, :, None, :, None]
    scores = (
        jnp.einsum("tahd,ubhd->hatbu", query, key_four, preferred_element_type=jnp.float32) * factor
    )
    scores = jnp.where(allowed, scores, -1e30)
    newest = jnp.maximum(running, jnp.max(scores, axis=(3, 4)))
    expo = jnp.where(allowed, jnp.exp(scores - newest[..., None, None]), 0.0)
    denom = jnp.sum(expo, axis=(3, 4))
    accum = jnp.einsum(
        "hatbu,ubhd->hatd",
        expo.astype(jnp.bfloat16),
        value_four,
        preferred_element_type=jnp.float32,
    )
    running, denom, accum = (newest, denom, accum)
    attended = (
        (accum / denom[..., None])
        .transpose(2, 1, 0, 3)
        .reshape(group_rows, span_count, head_count * HD)
        .astype(jnp.bfloat16)
    )
    rows = attended
    attn_sum = lax.psum_scatter(
        jnp.einsum("tck,kd->tcd", rows, out_weight, preferred_element_type=jnp.float32).astype(
            jnp.bfloat16
        ),
        "space",
        scatter_dimension=0,
        tiled=True,
    ).astype(jnp.float32)
    residual = (latents.astype(jnp.float32) + modulation[None, :, 2] * attn_sum).astype(
        jnp.bfloat16
    )
    second = norm_mod(
        lax.all_gather(residual, "space", axis=0, tiled=True).astype(jnp.float32),
        modulation[None, :, 3],
        modulation[None, :, 4],
    )
    hidden = jax.nn.gelu(
        jnp.einsum("tcd,df->tcf", second, up_weight, preferred_element_type=jnp.float32),
        approximate=True,
    ).astype(jnp.bfloat16)
    rows = hidden
    ffn_sum = lax.psum_scatter(
        jnp.einsum("tcf,fd->tcd", rows, down_weight, preferred_element_type=jnp.float32).astype(
            jnp.bfloat16
        ),
        "space",
        scatter_dimension=0,
        tiled=True,
    ).astype(jnp.float32)
    return (residual.astype(jnp.float32) + modulation[None, :, 5] * ffn_sum).astype(jnp.bfloat16)


def flip(index, bit):
    return index + bit * (1 - 2 * ((index // bit) % 2))


def layer_kernel(
    nz, ns, span_count, order_ref, key_span_ref, latent_ref, mod_ref, qkv_hbm, out_hbm, up_hbm, down_hbm,
    mixed_ref,
    x_ref, w_a, w_b, w_out, w_up, gathered, normed, query, kv, expo, scores, denom, attended, part,
    from_left, from_right, from_left2, from_right2, resid, hidden, acc, key_order_ref,
    w_sem, ag_send, ag_recv, kv_send, kv_recv, rs_send, rs_recv,
):
    z = lax.axis_index("space")
    me = lax.axis_index("span")
    rows, width = x_ref.shape
    whole = pl.ds(0, rows)
    tok = rows // span_count
    wide = width // CHUNKS
    last = nz - 1
    heads = query.shape[2] // HD
    down_blocks = width // BLOCK
    first_blocks = w_b.shape[0]

    def load(src, dst, slot):
        return pltpu.make_async_copy(src, dst, w_sem.at[slot])

    def columns(c, size):
        return pl.ds(c * size if isinstance(c, int) else pl.multiple_of(c * size, size), size)

    qkv_loads = [load(qkv_hbm.at[i], w_a.at[i], i) for i in range(3)]
    out_load = load(out_hbm, w_out, 3)
    up_loads = [load(up_hbm.at[:, columns(i, BLOCK)], w_up.at[i], 4 + i) for i in range(w_up.shape[0])]
    down_base = 4 + w_up.shape[0]
    down_loads = [
        load(
            down_hbm.at[:, columns(i, BLOCK)],
            w_b.at[i] if i < first_blocks else w_a.at[i - first_blocks],
            down_base + i,
        )
        for i in range(down_blocks)
    ]
    for i in (1, 2, 0):
        qkv_loads[i].start()
    stored = latent_ref[...].astype(jnp.float32)
    x_ref[...] = jnp.concatenate([stored[:, a, :] for a in range(span_count)], axis=0).astype(jnp.bfloat16)

    barrier = pltpu.get_barrier_semaphore()
    for bit in (1, 2, 4):
        pl.semaphore_signal(barrier, inc=1, device_id=(flip(me, bit), z), device_id_type=MESH)

    @pl.when(z > 0)
    def _():
        pl.semaphore_signal(barrier, inc=1, device_id=(me, z - 1), device_id_type=MESH)

    @pl.when(z < last)
    def _():
        pl.semaphore_signal(barrier, inc=1, device_id=(me, z + 1), device_id_type=MESH)

    pl.semaphore_wait(barrier, 3 + jnp.where(z > 0, 1, 0) + jnp.where(z < last, 1, 0))

    def ag_copy(which, way, s, c, src, dst):
        return pltpu.make_async_remote_copy(
            src_ref=src, dst_ref=dst,
            send_sem=ag_send.at[which, way, s, c], recv_sem=ag_recv.at[which, way, s, c],
            device_id=(me, z + 1 if way == 0 else z - 1), device_id_type=MESH,
        )

    def ag_sends(way, s):
        return jnp.logical_and(z < last, z - s >= 0) if way == 0 else jnp.logical_and(z > 0, z + s <= last)

    def ag_gets(way, s):
        return z - 1 - s >= 0 if way == 0 else z + 1 + s <= last

    def ag_own(which, own, buf, c, at):
        for way in range(2):
            @pl.when(ag_sends(way, 0))
            def _():
                ag_copy(
                    which, way, 0, c, own.at[at, columns(c, wide)], buf.at[z, at, columns(c, wide)]
                ).start()

    def ag_step(which, buf, s, c, at):
        for way in range(2):
            block = z - 1 - s if way == 0 else z + 1 + s

            @pl.when(ag_gets(way, s))
            def _():
                piece = buf.at[block, at, columns(c, wide)]
                ag_copy(which, way, s, c, piece, piece).wait_recv()

            if s + 1 < last:
                @pl.when(ag_sends(way, s + 1))
                def _():
                    piece = buf.at[block, at, columns(c, wide)]
                    ag_copy(which, way, s + 1, c, piece, piece).start()

    def ag_drain(which, buf, at):
        @pl.loop(0, CHUNKS)
        def _(c):
            for way in range(2):
                for s in range(last):
                    @pl.when(ag_sends(way, s))
                    def _():
                        piece = buf.at[0, at, columns(c, wide)]
                        ag_copy(which, way, s, c, piece, piece).wait_send()

    def segments(at):
        first, end = at.start, at.start + at.size
        runs = []
        for a in range(span_count):
            low, high = max(first, a * tok), min(end, (a + 1) * tok)
            if low < high:
                runs.append((a, low - first, high - first))
        return runs

    def norm_block(block, first, at):
        r = block.astype(jnp.float32)
        centred = r - jnp.mean(r, axis=-1, keepdims=True)
        variance = jnp.mean(centred * centred, axis=-1, keepdims=True)
        y = centred * lax.rsqrt(variance + 1e-06)
        pieces = []
        for a, low, high in segments(at):
            shift = mod_ref[first, a : a + 1, :]
            scale = mod_ref[first + 1, a : a + 1, :]
            pieces.append(y[low:high] * (1.0 + scale) + shift)
        return jnp.concatenate(pieces, axis=0).astype(jnp.bfloat16)

    def flip_all(index, rel):
        for bit in (1, 2, 4):
            if rel & bit:
                index = flip(index, bit)
        return index

    def kv_copy(which, rel, bit, block):
        piece = kv.at[which, flip_all(me, rel ^ bit), block]
        return pltpu.make_async_remote_copy(
            src_ref=piece, dst_ref=piece,
            send_sem=kv_send.at[which, rel, block], recv_sem=kv_recv.at[which, rel, block],
            device_id=(flip(me, bit), z), device_id_type=MESH,
        )

    def kv_take(which, rel, block):
        piece = kv.at[which, flip_all(me, rel), block]
        pltpu.make_async_remote_copy(
            src_ref=piece, dst_ref=piece,
            send_sem=kv_send.at[which, rel, block], recv_sem=kv_recv.at[which, rel, block],
            device_id=(flip(me, 1), z), device_id_type=MESH,
        ).wait_recv()

    def project(block, source, first):
        rows_in = norm_block(source, 0, whole)

        def part_of(i):
            if first:
                qkv_loads[i].wait()
            return jnp.dot(rows_in, w_a[i], preferred_element_type=jnp.float32).astype(jnp.bfloat16)

        for which in range(2):
            kv[which, me, block] = part_of(1 + which)
            for bit in ((2, 4, 1), (4, 2, 1))[which]:
                kv_copy(which, bit, bit, block).start()
        normed[block] = rows_in

    def second_hop(block):
        kv_take(0, 2, block)
        kv_copy(0, 6, 4, block).start()
        kv_copy(0, 3, 1, block).start()
        kv_take(1, 4, block)
        kv_copy(1, 6, 2, block).start()
        kv_copy(1, 5, 1, block).start()
        kv_take(0, 4, block)
        kv_copy(0, 5, 1, block).start()
        kv_take(1, 2, block)
        kv_copy(1, 3, 1, block).start()

    def third_hop(block):
        for which in range(2):
            kv_take(which, 6, block)
            kv_copy(which, 7, 1, block).start()

    def each_block(s, do):
        if s == -1:
            do(z)
        elif s >= 0:
            for way in range(2):
                @pl.when(ag_gets(way, s))
                def _():
                    do(z - 1 - s if way == 0 else z + 1 + s)

    @pl.loop(0, CHUNKS)
    def _(c):
        ag_own(0, x_ref, gathered, c, whole)

    out_load.start()
    for copy in up_loads:
        copy.start()
    for copy in down_loads[:first_blocks]:
        copy.start()
    project(z, x_ref[...], True)
    for s in range(last):
        @pl.loop(0, CHUNKS)
        def _(c):
            ag_step(0, gathered, s, c, whole)

        each_block(s, lambda block: project(block, gathered[block], False))
        each_block(s - 1, second_hop)
        each_block(s - 2, third_hop)
    each_block(last - 1, second_hop)
    qkv_loads[0].wait()
    query[...] = (
        jnp.dot(normed[...].reshape(nz * rows, width), w_a[0], preferred_element_type=jnp.float32)
        .astype(jnp.bfloat16)
        .reshape(query.shape)
    )
    for copy in down_loads[first_blocks:]:
        copy.start()
    each_block(last - 2, third_hop)
    each_block(last - 1, third_hop)
    ag_drain(0, gathered, whole)

    @pl.loop(0, nz)
    def _(block):
        for which in range(2):
            for rel in (1, 3, 5, 7):
                kv_take(which, rel, block)

    total_rows = nz * rows
    keys_rows = ns * total_rows
    factor = 1.0 / HD**0.5
    places = [order_ref[me * span_count + a] for a in range(span_count)]

    key_order = jnp.zeros((1, keys_rows), jnp.int32)
    for span in range(ns * span_count):
        key_order = jnp.where(key_span_ref[...] == span, order_ref[span], key_order)
    key_order_ref[...] = key_order

    def head_scores(h):
        key_order = key_order_ref[...]
        lanes = pl.ds(pl.multiple_of(h * HD, HD), HD)
        keys = kv[0, :, :, :, lanes].reshape(keys_rows, HD)
        scores[...] = lax.dot_general(
            query[:, :, lanes].reshape(total_rows, HD), keys, (((1,), (1,)), ((), ())), preferred_element_type=jnp.float32
        )
        for block in range(nz):
            out = []
            sums = []
            for a in range(span_count):
                at = block * rows + a * tok
                allowed = key_order <= places[a]
                sc = jnp.where(allowed, scores[at : at + tok, :] * factor, -1e30)
                e = jnp.exp(sc - jnp.max(sc, axis=-1, keepdims=True))
                e = jnp.where(allowed, e, 0.0)
                out.append(e)
                sums.append(jnp.broadcast_to(jnp.sum(e, axis=-1, keepdims=True), (tok, HD)))
            expo[h, block * rows : (block + 1) * rows, :] = jnp.concatenate(out, axis=0).astype(jnp.bfloat16)
            denom[h, block * rows : (block + 1) * rows, :] = jnp.concatenate(sums, axis=0)

    @pl.loop(0, heads)
    def _(h):
        head_scores(h)

    @pl.loop(0, heads)
    def _(h):
        lanes = pl.ds(pl.multiple_of(h * HD, HD), HD)
        mixed_values = jnp.dot(
            expo[h], kv[1, :, :, :, lanes].reshape(keys_rows, HD), preferred_element_type=jnp.float32
        )
        attended[:, lanes] = (mixed_values / denom[h]).astype(jnp.bfloat16)

    @pl.loop(0, nz)
    def _(block):
        for which in range(2):
            for rel in range(1, 8):
                bit = rel & -rel if rel != 6 else (4 if which == 0 else 2)
                kv_copy(which, rel, bit, block).wait_send()

    def rs_buf(stage, way):
        return ((from_left, from_right), (from_left2, from_right2))[stage][way]

    def rs_copy(stage, way, s, c, owner):
        return pltpu.make_async_remote_copy(
            src_ref=part.at[owner, :, columns(c, wide)],
            dst_ref=rs_buf(stage, way).at[owner, :, columns(c, wide)],
            send_sem=rs_send.at[stage, way, s, c], recv_sem=rs_recv.at[stage, way, s, c],
            device_id=(me, z + 1 if way == 0 else z - 1), device_id_type=MESH,
        )

    def rs_start(stage, c):
        @pl.when(z == 0)
        def _():
            for s in range(last):
                rs_copy(stage, 0, s, c, last - s).start()

        @pl.when(z == last)
        def _():
            for s in range(last):
                rs_copy(stage, 1, s, c, s).start()

    def live(c):
        return jnp.logical_and(c >= 0, c < CHUNKS)

    def farther(at):
        return jnp.where(2 * at > last, at, last - at)

    def rs_tick(stage, t, then):
        for way in range(2):
            c = t + 1 - z if way == 0 else t + 1 - last + z
            inner = z > 0 if way == 0 else z < last
            for s in range(last):
                owner = last - s if way == 0 else s
                beyond = owner > z if way == 0 else owner < z

                @pl.when(jnp.logical_and(jnp.logical_and(inner, beyond), live(c)))
                def _():
                    cols = columns(c, wide)
                    copy = rs_copy(stage, way, s, c, owner)
                    copy.wait_recv()
                    part[owner, :, cols] = (
                        part[owner, :, cols].astype(jnp.float32)
                        + rs_buf(stage, way)[owner, :, cols].astype(jnp.float32)
                    ).astype(jnp.bfloat16)
                    copy.start()

        own = t + 1 - farther(z)

        @pl.when(live(own))
        def _():
            cols = columns(own, wide)
            acc[...] = part[z, :, cols].astype(jnp.float32)

            @pl.when(z > 0)
            def _():
                rs_copy(stage, 0, last - z, own, z).wait_recv()
                acc[...] += rs_buf(stage, 0)[z, :, cols].astype(jnp.float32)

            @pl.when(z < last)
            def _():
                rs_copy(stage, 1, z, own, z).wait_recv()
                acc[...] += rs_buf(stage, 1)[z, :, cols].astype(jnp.float32)

            then(own)

    def rs_drain(stage):
        @pl.loop(0, CHUNKS)
        def _(c):
            for s in range(last):
                for way in range(2):
                    owner = last - s if way == 0 else s

                    @pl.when(owner > z if way == 0 else owner < z)
                    def _():
                        rs_copy(stage, way, s, c, owner).wait_send()

    def ag_tick(t):
        for way in range(2):
            for s in range(last):
                block = z - 1 - s if way == 0 else z + 1 + s
                c = t - farther(block) - s

                @pl.when(jnp.logical_and(ag_gets(way, s), live(c)))
                def _():
                    piece = resid.at[block, :, columns(c, wide)]
                    ag_copy(1, way, s, c, piece, piece).wait_recv()
                    if s + 1 < last:
                        @pl.when(ag_sends(way, s + 1))
                        def _():
                            ag_copy(1, way, s + 1, c, piece, piece).start()

    def gated(base, gate, c):
        base = base.astype(jnp.float32)
        pieces = []
        for a, low, high in segments(whole):
            row = mod_ref[gate, a : a + 1, columns(c, wide)]
            pieces.append(base[low:high] + row * acc[low:high, :])
        return jnp.concatenate(pieces, axis=0).astype(jnp.bfloat16)

    def to_residual(c):
        cols = columns(c, wide)
        resid[z, :, cols] = gated(x_ref[:, cols], 2, c)
        ag_own(1, resid.at[z], resid, c, whole)

    def to_mixed(c):
        cols = columns(c, wide)
        mixed_ref[:, cols] = gated(resid[z, :, cols], 5, c)

    out_load.wait()

    @pl.loop(0, CHUNKS)
    def _(c):
        part[:, :, columns(c, wide)] = (
            jnp.dot(attended[...], w_out[:, columns(c, wide)], preferred_element_type=jnp.float32)
            .astype(jnp.bfloat16)
            .reshape(nz, rows, wide)
        )
        rs_start(0, c)

    @pl.loop(0, CHUNKS + 2 * last - 1)
    def _(t):
        rs_tick(0, t, to_residual)
        ag_tick(t)

    @pl.loop(0, nz)
    def _(block):
        normed[block] = norm_block(resid[block], 3, whole)

    for copy in up_loads:
        copy.wait()

    @pl.loop(0, w_up.shape[0])
    def _(i):
        raised = jnp.dot(
            normed[...].reshape(total_rows, width), w_up[i], preferred_element_type=jnp.float32
        )
        hidden[:, columns(i, BLOCK)] = jax.nn.gelu(raised, approximate=True).astype(jnp.bfloat16)

    ag_drain(1, resid, whole)
    rs_drain(0)
    for i in range(down_blocks):
        down_loads[i].wait()
        weight = w_b[i] if i < first_blocks else w_a[i - first_blocks]
        part[:, :, columns(i, BLOCK)] = (
            jnp.dot(hidden[...], weight, preferred_element_type=jnp.float32)
            .astype(jnp.bfloat16)
            .reshape(nz, rows, BLOCK)
        )
        rs_start(1, i)
        if i > 0:
            rs_tick(1, i - 1, to_mixed)

    @pl.loop(CHUNKS - 1, CHUNKS + last - 1)
    def _(t):
        rs_tick(1, t, to_mixed)

    rs_drain(1)


def kernel_body(nz, ns, latents, span_order, modulation, qkv_weight, out_weight, up_weight, down_weight):
    tok, span_count, width = latents.shape
    rows = tok * span_count
    total = rows * nz
    head_cols = qkv_weight.shape[2]
    heads = head_cols // HD
    hid = up_weight.shape[1]
    keys_rows = ns * total
    key_span = np.broadcast_to(
        np.arange(ns * span_count, dtype=np.int32).reshape(ns, 1, span_count, 1), (ns, nz, span_count, tok)
    ).reshape(1, keys_rows)
    blocks = width // BLOCK
    later = qkv_weight.shape[0]
    bf, f32 = jnp.bfloat16, jnp.float32
    vmem = pl.BlockSpec(memory_space=pltpu.VMEM)
    hbm = pl.BlockSpec(memory_space=pl.ANY)
    grouped = pltpu.VMEM((nz, rows, width), bf)
    flops = 2 * total * width * (4 * head_cols + 2 * hid) + 4 * total * keys_rows * head_cols
    mixed = pl.pallas_call(
        functools.partial(layer_kernel, nz, ns, span_count),
        out_shape=jax.ShapeDtypeStruct((rows, width), bf),
        in_specs=[pl.BlockSpec(memory_space=pltpu.SMEM), vmem, vmem, vmem, hbm, hbm, hbm, hbm],
        out_specs=vmem,
        scratch_shapes=[
            pltpu.VMEM((rows, width), bf),
            pltpu.VMEM((later, width, head_cols), bf),
            pltpu.VMEM((blocks - later, hid, BLOCK), bf),
            pltpu.VMEM((head_cols, width), bf),
            pltpu.VMEM((hid // BLOCK, width, BLOCK), bf),
            grouped,
            grouped,
            pltpu.VMEM((nz, rows, head_cols), bf),
            pltpu.VMEM((2, ns, nz, rows, head_cols), bf),
            pltpu.VMEM((heads, total, keys_rows), bf),
            pltpu.VMEM((total, keys_rows), f32),
            pltpu.VMEM((heads, total, HD), f32),
            pltpu.VMEM((total, head_cols), bf),
            grouped,
            grouped,
            grouped,
            grouped,
            grouped,
            grouped,
            pltpu.VMEM((total, hid), bf),
            pltpu.VMEM((rows, width // CHUNKS), f32),
            pltpu.VMEM((1, keys_rows), jnp.int32),
            pltpu.SemaphoreType.DMA((4 + hid // BLOCK + blocks,)),
            pltpu.SemaphoreType.DMA((2, 2, nz - 1, CHUNKS)),
            pltpu.SemaphoreType.DMA((2, 2, nz - 1, CHUNKS)),
            pltpu.SemaphoreType.DMA((2, ns, nz)),
            pltpu.SemaphoreType.DMA((2, ns, nz)),
            pltpu.SemaphoreType.DMA((2, 2, nz - 1, CHUNKS)),
            pltpu.SemaphoreType.DMA((2, 2, nz - 1, CHUNKS)),
        ],
        compiler_params=pltpu.CompilerParams(
            collective_id=0, has_side_effects=True, vmem_limit_bytes=VMEM_BYTES
        ),
        cost_estimate=pl.CostEstimate(
            flops=flops,
            bytes_accessed=2 * width * (4 * head_cols + 2 * hid),
            transcendentals=total * (keys_rows * heads + hid),
        ),
    )(span_order, key_span, latents, modulation.transpose(1, 0, 2), qkv_weight, out_weight, up_weight, down_weight)
    return mixed.reshape(span_count, tok, width).transpose(1, 0, 2)


def fits(nz, ns, tok, span_count, width, head_cols, hid):
    rows = tok * span_count
    total = rows * nz
    keys_rows = ns * total
    weights = 2 * width * (4 * head_cols + 2 * hid) - 2 * width * 3 * head_cols
    moving = 2 * (9 * total * width + 2 * (keys_rows + total) * head_cols)
    moving += 2 * total * keys_rows * (head_cols // HD + 2) + 4 * total * head_cols
    return (
        ns == 8
        and nz > 1
        and rows % 16 == 0
        and tok % 8 == 0
        and head_cols == BLOCK
        and width == hid
        and width == CHUNKS * BLOCK
        and weights + moving < VMEM_BYTES
    )


def body(nz, ns, latents, span_order, modulation, qkv_weight, out_weight, up_weight, down_weight):
    args = (latents, span_order, modulation, qkv_weight, out_weight, up_weight, down_weight)
    if fits(nz, ns, *latents.shape, qkv_weight.shape[2], up_weight.shape[1]):
        return kernel_body(nz, ns, *args)
    return plain_body(*args)


def solution(mesh):
    return jax.shard_map(
        functools.partial(body, mesh.shape["space"], mesh.shape["span"]),
        mesh=mesh,
        in_specs=(
            P("space", "span", None),
            P(),
            P("span", None, None),
            P(None, None, "space"),
            P("space", None),
            P(None, "space"),
            P("space", None),
        ),
        out_specs=P("space", "span", None),
        check_vma=False,
    )
```

```python
import functools

import jax
import jax.numpy as jnp
import numpy as np
from jax import lax
from jax.experimental import pallas as pl
from jax.experimental.pallas import tpu as pltpu
from jax.sharding import PartitionSpec as P

HD = 128
CHUNKS = 6
BLOCK = 512
MESH = pl.DeviceIdType.MESH
VMEM_BYTES = 62 * 1024 * 1024


def norm_mod(rows, shift, scale):
    mean = jnp.mean(rows, axis=-1, keepdims=True)
    centred = rows - mean
    variance = jnp.mean(centred * centred, axis=-1, keepdims=True)
    return (centred * lax.rsqrt(variance + 1e-06) * (1.0 + scale) + shift).astype(jnp.bfloat16)


def plain_body(latents, span_order, modulation, qkv_weight, out_weight, up_weight, down_weight):
    span_count = latents.shape[1]
    head_count = qkv_weight.shape[2] // HD
    my_start = lax.axis_index("span") * span_count
    my_places = lax.dynamic_slice_in_dim(span_order, my_start, span_count, 0)
    gathered = lax.all_gather(latents, "space", axis=0, tiled=True)
    group_rows = gathered.shape[0]
    gathered_f = gathered.astype(jnp.float32)
    normed = norm_mod(gathered_f, modulation[None, :, 0], modulation[None, :, 1])
    projected = jnp.einsum(
        "tcd,sdf->stcf", normed, qkv_weight, preferred_element_type=jnp.float32
    ).astype(jnp.bfloat16)
    query = projected[0].reshape(group_rows, span_count, head_count, HD)
    factor = 1.0 / HD**0.5
    running = jnp.full((head_count, span_count, group_rows), -1e30, jnp.float32)
    key_piece = lax.all_gather(projected[1], "span", axis=1, tiled=True)
    value_piece = lax.all_gather(projected[2], "span", axis=1, tiled=True)
    piece_spans = key_piece.shape[1]
    key_four = key_piece.reshape(group_rows, piece_spans, head_count, HD)
    value_four = value_piece.reshape(group_rows, piece_spans, head_count, HD)
    allowed = (span_order[None, :] <= my_places[:, None])[None, :, None, :, None]
    scores = (
        jnp.einsum("tahd,ubhd->hatbu", query, key_four, preferred_element_type=jnp.float32) * factor
    )
    scores = jnp.where(allowed, scores, -1e30)
    newest = jnp.maximum(running, jnp.max(scores, axis=(3, 4)))
    expo = jnp.where(allowed, jnp.exp(scores - newest[..., None, None]), 0.0)
    denom = jnp.sum(expo, axis=(3, 4))
    accum = jnp.einsum(
        "hatbu,ubhd->hatd",
        expo.astype(jnp.bfloat16),
        value_four,
        preferred_element_type=jnp.float32,
    )
    running, denom, accum = (newest, denom, accum)
    attended = (
        (accum / denom[..., None])
        .transpose(2, 1, 0, 3)
        .reshape(group_rows, span_count, head_count * HD)
        .astype(jnp.bfloat16)
    )
    rows = attended
    attn_sum = lax.psum_scatter(
        jnp.einsum("tck,kd->tcd", rows, out_weight, preferred_element_type=jnp.float32).astype(
            jnp.bfloat16
        ),
        "space",
        scatter_dimension=0,
        tiled=True,
    ).astype(jnp.float32)
    residual = (latents.astype(jnp.float32) + modulation[None, :, 2] * attn_sum).astype(
        jnp.bfloat16
    )
    second = norm_mod(
        lax.all_gather(residual, "space", axis=0, tiled=True).astype(jnp.float32),
        modulation[None, :, 3],
        modulation[None, :, 4],
    )
    hidden = jax.nn.gelu(
        jnp.einsum("tcd,df->tcf", second, up_weight, preferred_element_type=jnp.float32),
        approximate=True,
    ).astype(jnp.bfloat16)
    rows = hidden
    ffn_sum = lax.psum_scatter(
        jnp.einsum("tcf,fd->tcd", rows, down_weight, preferred_element_type=jnp.float32).astype(
            jnp.bfloat16
        ),
        "space",
        scatter_dimension=0,
        tiled=True,
    ).astype(jnp.float32)
    return (residual.astype(jnp.float32) + modulation[None, :, 5] * ffn_sum).astype(jnp.bfloat16)


def flip(index, bit):
    return index + bit * (1 - 2 * ((index // bit) % 2))


def layer_kernel(
    nz, ns, span_count, order_ref, key_span_ref, latent_ref, mod_ref, qkv_hbm, out_hbm, up_hbm, down_hbm,
    mixed_ref,
    x_ref, w_a, w_b, w_out, w_up, gathered, normed, query, kv, expo, scores, denom, attended, part,
    from_left, from_right, from_left2, from_right2, resid, hidden, acc, key_order_ref,
    w_sem, ag_send, ag_recv, kv_send, kv_recv, rs_send, rs_recv,
):
    z = lax.axis_index("space")
    me = lax.axis_index("span")
    rows, width = x_ref.shape
    whole = pl.ds(0, rows)
    tok = rows // span_count
    wide = width // CHUNKS
    last = nz - 1
    heads = query.shape[2] // HD
    down_blocks = width // BLOCK
    first_blocks = w_b.shape[0]

    def load(src, dst, slot):
        return pltpu.make_async_copy(src, dst, w_sem.at[slot])

    def columns(c, size):
        return pl.ds(c * size if isinstance(c, int) else pl.multiple_of(c * size, size), size)

    qkv_loads = [load(qkv_hbm.at[i], w_a.at[i], i) for i in range(3)]
    out_load = load(out_hbm, w_out, 3)
    up_loads = [load(up_hbm.at[:, columns(i, BLOCK)], w_up.at[i], 4 + i) for i in range(w_up.shape[0])]
    down_base = 4 + w_up.shape[0]
    down_loads = [
        load(
            down_hbm.at[:, columns(i, BLOCK)],
            w_b.at[i] if i < first_blocks else w_a.at[i - first_blocks],
            down_base + i,
        )
        for i in range(down_blocks)
    ]
    for i in (1, 2, 0):
        qkv_loads[i].start()
    stored = latent_ref[...].astype(jnp.float32)
    x_ref[...] = jnp.concatenate([stored[:, a, :] for a in range(span_count)], axis=0).astype(jnp.bfloat16)

    barrier = pltpu.get_barrier_semaphore()
    for bit in (1, 2, 4):
        pl.semaphore_signal(barrier, inc=1, device_id=(flip(me, bit), z), device_id_type=MESH)

    @pl.when(z > 0)
    def _():
        pl.semaphore_signal(barrier, inc=1, device_id=(me, z - 1), device_id_type=MESH)

    @pl.when(z < last)
    def _():
        pl.semaphore_signal(barrier, inc=1, device_id=(me, z + 1), device_id_type=MESH)

    pl.semaphore_wait(barrier, 3 + jnp.where(z > 0, 1, 0) + jnp.where(z < last, 1, 0))

    def ag_copy(which, way, s, c, src, dst):
        return pltpu.make_async_remote_copy(
            src_ref=src, dst_ref=dst,
            send_sem=ag_send.at[which, way, s, c], recv_sem=ag_recv.at[which, way, s, c],
            device_id=(me, z + 1 if way == 0 else z - 1), device_id_type=MESH,
        )

    def ag_sends(way, s):
        return jnp.logical_and(z < last, z - s >= 0) if way == 0 else jnp.logical_and(z > 0, z + s <= last)

    def ag_gets(way, s):
        return z - 1 - s >= 0 if way == 0 else z + 1 + s <= last

    def ag_own(which, own, buf, c, at):
        for way in range(2):
            @pl.when(ag_sends(way, 0))
            def _():
                ag_copy(
                    which, way, 0, c, own.at[at, columns(c, wide)], buf.at[z, at, columns(c, wide)]
                ).start()

    def ag_step(which, buf, s, c, at):
        for way in range(2):
            block = z - 1 - s if way == 0 else z + 1 + s

            @pl.when(ag_gets(way, s))
            def _():
                piece = buf.at[block, at, columns(c, wide)]
                ag_copy(which, way, s, c, piece, piece).wait_recv()

            if s + 1 < last:
                @pl.when(ag_sends(way, s + 1))
                def _():
                    piece = buf.at[block, at, columns(c, wide)]
                    ag_copy(which, way, s + 1, c, piece, piece).start()

    def ag_drain(which, buf, at):
        @pl.loop(0, CHUNKS)
        def _(c):
            for way in range(2):
                for s in range(last):
                    @pl.when(ag_sends(way, s))
                    def _():
                        piece = buf.at[0, at, columns(c, wide)]
                        ag_copy(which, way, s, c, piece, piece).wait_send()

    def segments(at):
        first, end = at.start, at.start + at.size
        runs = []
        for a in range(span_count):
            low, high = max(first, a * tok), min(end, (a + 1) * tok)
            if low < high:
                runs.append((a, low - first, high - first))
        return runs

    def norm_block(block, first, at):
        r = block.astype(jnp.float32)
        centred = r - jnp.mean(r, axis=-1, keepdims=True)
        variance = jnp.mean(centred * centred, axis=-1, keepdims=True)
        y = centred * lax.rsqrt(variance + 1e-06)
        pieces = []
        for a, low, high in segments(at):
            shift = mod_ref[first, a : a + 1, :]
            scale = mod_ref[first + 1, a : a + 1, :]
            pieces.append(y[low:high] * (1.0 + scale) + shift)
        return jnp.concatenate(pieces, axis=0).astype(jnp.bfloat16)

    def flip_all(index, rel):
        for bit in (1, 2, 4):
            if rel & bit:
                index = flip(index, bit)
        return index

    def kv_copy(which, rel, bit, block):
        piece = kv.at[which, flip_all(me, rel ^ bit), block]
        return pltpu.make_async_remote_copy(
            src_ref=piece, dst_ref=piece,
            send_sem=kv_send.at[which, rel, block], recv_sem=kv_recv.at[which, rel, block],
            device_id=(flip(me, bit), z), device_id_type=MESH,
        )

    def kv_take(which, rel, block):
        piece = kv.at[which, flip_all(me, rel), block]
        pltpu.make_async_remote_copy(
            src_ref=piece, dst_ref=piece,
            send_sem=kv_send.at[which, rel, block], recv_sem=kv_recv.at[which, rel, block],
            device_id=(flip(me, 1), z), device_id_type=MESH,
        ).wait_recv()

    def project(block, source, first):
        rows_in = norm_block(source, 0, whole)

        def part_of(i):
            if first:
                qkv_loads[i].wait()
            return jnp.dot(rows_in, w_a[i], preferred_element_type=jnp.float32).astype(jnp.bfloat16)

        for which in range(2):
            kv[which, me, block] = part_of(1 + which)
            for bit in ((2, 4, 1), (4, 2, 1))[which]:
                kv_copy(which, bit, bit, block).start()
        normed[block] = rows_in

    def second_hop(block):
        kv_take(0, 2, block)
        kv_copy(0, 6, 4, block).start()
        kv_copy(0, 3, 1, block).start()
        kv_take(1, 4, block)
        kv_copy(1, 6, 2, block).start()
        kv_copy(1, 5, 1, block).start()
        kv_take(0, 4, block)
        kv_copy(0, 5, 1, block).start()
        kv_take(1, 2, block)
        kv_copy(1, 3, 1, block).start()

    def third_hop(block):
        for which in range(2):
            kv_take(which, 6, block)
            kv_copy(which, 7, 1, block).start()

    def each_block(s, do):
        if s == -1:
            do(z)
        elif s >= 0:
            for way in range(2):
                @pl.when(ag_gets(way, s))
                def _():
                    do(z - 1 - s if way == 0 else z + 1 + s)

    @pl.loop(0, CHUNKS)
    def _(c):
        ag_own(0, x_ref, gathered, c, whole)

    out_load.start()
    for copy in up_loads:
        copy.start()
    for copy in down_loads[:first_blocks]:
        copy.start()
    project(z, x_ref[...], True)
    for s in range(last):
        @pl.loop(0, CHUNKS)
        def _(c):
            ag_step(0, gathered, s, c, whole)

        each_block(s, lambda block: project(block, gathered[block], False))
        each_block(s - 1, second_hop)
        each_block(s - 2, third_hop)
    each_block(last - 1, second_hop)
    qkv_loads[0].wait()
    query[...] = (
        jnp.dot(normed[...].reshape(nz * rows, width), w_a[0], preferred_element_type=jnp.float32)
        .astype(jnp.bfloat16)
        .reshape(query.shape)
    )
    for copy in down_loads[first_blocks:]:
        copy.start()
    each_block(last - 2, third_hop)
    each_block(last - 1, third_hop)
    ag_drain(0, gathered, whole)

    @pl.loop(0, nz)
    def _(block):
        for which in range(2):
            for rel in (1, 3, 5, 7):
                kv_take(which, rel, block)

    total_rows = nz * rows
    keys_rows = ns * total_rows
    factor = 1.0 / HD**0.5
    places = [order_ref[me * span_count + a] for a in range(span_count)]

    key_order = jnp.zeros((1, keys_rows), jnp.int32)
    for span in range(ns * span_count):
        key_order = jnp.where(key_span_ref[...] == span, order_ref[span], key_order)
    key_order_ref[...] = key_order

    def head_scores(h):
        key_order = key_order_ref[...]
        lanes = pl.ds(h * HD, HD)
        keys = kv[0, :, :, :, lanes].reshape(keys_rows, HD)
        scores[h] = lax.dot_general(
            query[:, :, lanes].reshape(total_rows, HD), keys, (((1,), (1,)), ((), ())), preferred_element_type=jnp.float32
        )
        for block in range(nz):
            out = []
            sums = []
            for a in range(span_count):
                at = block * rows + a * tok
                allowed = key_order <= places[a]
                sc = jnp.where(allowed, scores[h, at : at + tok, :] * factor, -1e30)
                e = jnp.exp(sc - jnp.max(sc, axis=-1, keepdims=True))
                e = jnp.where(allowed, e, 0.0)
                out.append(e)
                sums.append(jnp.broadcast_to(jnp.sum(e, axis=-1, keepdims=True), (tok, HD)))
            expo[h, block * rows : (block + 1) * rows, :] = jnp.concatenate(out, axis=0).astype(jnp.bfloat16)
            denom[h, block * rows : (block + 1) * rows, :] = jnp.concatenate(sums, axis=0)

    def head_values(h):
        lanes = pl.ds(h * HD, HD)
        mixed_values = jnp.dot(
            expo[h], kv[1, :, :, :, lanes].reshape(keys_rows, HD), preferred_element_type=jnp.float32
        )
        attended[:, lanes] = (mixed_values / denom[h]).astype(jnp.bfloat16)

    for h in range(heads):
        head_scores(h)
    for h in range(heads):
        head_values(h)

    @pl.loop(0, nz)
    def _(block):
        for which in range(2):
            for rel in range(1, 8):
                bit = rel & -rel if rel != 6 else (4 if which == 0 else 2)
                kv_copy(which, rel, bit, block).wait_send()

    def rs_buf(stage, way):
        return ((from_left, from_right), (from_left2, from_right2))[stage][way]

    def rs_copy(stage, way, s, c, owner):
        return pltpu.make_async_remote_copy(
            src_ref=part.at[owner, :, columns(c, wide)],
            dst_ref=rs_buf(stage, way).at[owner, :, columns(c, wide)],
            send_sem=rs_send.at[stage, way, s, c], recv_sem=rs_recv.at[stage, way, s, c],
            device_id=(me, z + 1 if way == 0 else z - 1), device_id_type=MESH,
        )

    def rs_start(stage, c):
        @pl.when(z == 0)
        def _():
            for s in range(last):
                rs_copy(stage, 0, s, c, last - s).start()

        @pl.when(z == last)
        def _():
            for s in range(last):
                rs_copy(stage, 1, s, c, s).start()

    def live(c):
        return jnp.logical_and(c >= 0, c < CHUNKS)

    def farther(at):
        return jnp.where(2 * at > last, at, last - at)

    def rs_tick(stage, t, then):
        for way in range(2):
            c = t + 1 - z if way == 0 else t + 1 - last + z
            inner = z > 0 if way == 0 else z < last
            for s in range(last):
                owner = last - s if way == 0 else s
                beyond = owner > z if way == 0 else owner < z

                @pl.when(jnp.logical_and(jnp.logical_and(inner, beyond), live(c)))
                def _():
                    cols = columns(c, wide)
                    copy = rs_copy(stage, way, s, c, owner)
                    copy.wait_recv()
                    part[owner, :, cols] = (
                        part[owner, :, cols].astype(jnp.float32)
                        + rs_buf(stage, way)[owner, :, cols].astype(jnp.float32)
                    ).astype(jnp.bfloat16)
                    copy.start()

        own = t + 1 - farther(z)

        @pl.when(live(own))
        def _():
            cols = columns(own, wide)
            acc[...] = part[z, :, cols].astype(jnp.float32)

            @pl.when(z > 0)
            def _():
                rs_copy(stage, 0, last - z, own, z).wait_recv()
                acc[...] += rs_buf(stage, 0)[z, :, cols].astype(jnp.float32)

            @pl.when(z < last)
            def _():
                rs_copy(stage, 1, z, own, z).wait_recv()
                acc[...] += rs_buf(stage, 1)[z, :, cols].astype(jnp.float32)

            then(own)

    def rs_drain(stage):
        @pl.loop(0, CHUNKS)
        def _(c):
            for s in range(last):
                for way in range(2):
                    owner = last - s if way == 0 else s

                    @pl.when(owner > z if way == 0 else owner < z)
                    def _():
                        rs_copy(stage, way, s, c, owner).wait_send()

    def ag_tick(t):
        for way in range(2):
            for s in range(last):
                block = z - 1 - s if way == 0 else z + 1 + s
                c = t - farther(block) - s

                @pl.when(jnp.logical_and(ag_gets(way, s), live(c)))
                def _():
                    piece = resid.at[block, :, columns(c, wide)]
                    ag_copy(1, way, s, c, piece, piece).wait_recv()
                    if s + 1 < last:
                        @pl.when(ag_sends(way, s + 1))
                        def _():
                            ag_copy(1, way, s + 1, c, piece, piece).start()

    def gated(base, gate, c):
        base = base.astype(jnp.float32)
        pieces = []
        for a, low, high in segments(whole):
            row = mod_ref[gate, a : a + 1, columns(c, wide)]
            pieces.append(base[low:high] + row * acc[low:high, :])
        return jnp.concatenate(pieces, axis=0).astype(jnp.bfloat16)

    def to_residual(c):
        cols = columns(c, wide)
        resid[z, :, cols] = gated(x_ref[:, cols], 2, c)
        ag_own(1, resid.at[z], resid, c, whole)

    def to_mixed(c):
        cols = columns(c, wide)
        mixed_ref[:, cols] = gated(resid[z, :, cols], 5, c)

    out_load.wait()

    @pl.loop(0, CHUNKS)
    def _(c):
        part[:, :, columns(c, wide)] = (
            jnp.dot(attended[...], w_out[:, columns(c, wide)], preferred_element_type=jnp.float32)
            .astype(jnp.bfloat16)
            .reshape(nz, rows, wide)
        )
        rs_start(0, c)

    @pl.loop(0, CHUNKS + 2 * last - 1)
    def _(t):
        rs_tick(0, t, to_residual)
        ag_tick(t)

    @pl.loop(0, nz)
    def _(block):
        normed[block] = norm_block(resid[block], 3, whole)

    for copy in up_loads:
        copy.wait()

    for i in range(w_up.shape[0]):
        raised = jnp.dot(
            normed[...].reshape(total_rows, width), w_up[i], preferred_element_type=jnp.float32
        )
        hidden[:, columns(i, BLOCK)] = jax.nn.gelu(raised, approximate=True).astype(jnp.bfloat16)

    ag_drain(1, resid, whole)
    rs_drain(0)
    for i in range(down_blocks):
        down_loads[i].wait()
        weight = w_b[i] if i < first_blocks else w_a[i - first_blocks]
        part[:, :, columns(i, BLOCK)] = (
            jnp.dot(hidden[...], weight, preferred_element_type=jnp.float32)
            .astype(jnp.bfloat16)
            .reshape(nz, rows, BLOCK)
        )
        rs_start(1, i)
        if i > 0:
            rs_tick(1, i - 1, to_mixed)

    @pl.loop(CHUNKS - 1, CHUNKS + last - 1)
    def _(t):
        rs_tick(1, t, to_mixed)

    rs_drain(1)


def kernel_body(nz, ns, latents, span_order, modulation, qkv_weight, out_weight, up_weight, down_weight):
    tok, span_count, width = latents.shape
    rows = tok * span_count
    total = rows * nz
    head_cols = qkv_weight.shape[2]
    heads = head_cols // HD
    hid = up_weight.shape[1]
    keys_rows = ns * total
    key_span = np.broadcast_to(
        np.arange(ns * span_count, dtype=np.int32).reshape(ns, 1, span_count, 1), (ns, nz, span_count, tok)
    ).reshape(1, keys_rows)
    blocks = width // BLOCK
    later = qkv_weight.shape[0]
    bf, f32 = jnp.bfloat16, jnp.float32
    vmem = pl.BlockSpec(memory_space=pltpu.VMEM)
    hbm = pl.BlockSpec(memory_space=pl.ANY)
    grouped = pltpu.VMEM((nz, rows, width), bf)
    flops = 2 * total * width * (4 * head_cols + 2 * hid) + 4 * total * keys_rows * head_cols
    mixed = pl.pallas_call(
        functools.partial(layer_kernel, nz, ns, span_count),
        out_shape=jax.ShapeDtypeStruct((rows, width), bf),
        in_specs=[pl.BlockSpec(memory_space=pltpu.SMEM), vmem, vmem, vmem, hbm, hbm, hbm, hbm],
        out_specs=vmem,
        scratch_shapes=[
            pltpu.VMEM((rows, width), bf),
            pltpu.VMEM((later, width, head_cols), bf),
            pltpu.VMEM((blocks - later, hid, BLOCK), bf),
            pltpu.VMEM((head_cols, width), bf),
            pltpu.VMEM((hid // BLOCK, width, BLOCK), bf),
            grouped,
            grouped,
            pltpu.VMEM((nz, rows, head_cols), bf),
            pltpu.VMEM((2, ns, nz, rows, head_cols), bf),
            pltpu.VMEM((heads, total, keys_rows), bf),
            pltpu.VMEM((heads, total, keys_rows), f32),
            pltpu.VMEM((heads, total, HD), f32),
            pltpu.VMEM((total, head_cols), bf),
            grouped,
            grouped,
            grouped,
            grouped,
            grouped,
            grouped,
            pltpu.VMEM((total, hid), bf),
            pltpu.VMEM((rows, width // CHUNKS), f32),
            pltpu.VMEM((1, keys_rows), jnp.int32),
            pltpu.SemaphoreType.DMA((4 + hid // BLOCK + blocks,)),
            pltpu.SemaphoreType.DMA((2, 2, nz - 1, CHUNKS)),
            pltpu.SemaphoreType.DMA((2, 2, nz - 1, CHUNKS)),
            pltpu.SemaphoreType.DMA((2, ns, nz)),
            pltpu.SemaphoreType.DMA((2, ns, nz)),
            pltpu.SemaphoreType.DMA((2, 2, nz - 1, CHUNKS)),
            pltpu.SemaphoreType.DMA((2, 2, nz - 1, CHUNKS)),
        ],
        compiler_params=pltpu.CompilerParams(
            collective_id=0, has_side_effects=True, vmem_limit_bytes=VMEM_BYTES
        ),
        cost_estimate=pl.CostEstimate(
            flops=flops,
            bytes_accessed=2 * width * (4 * head_cols + 2 * hid),
            transcendentals=total * (keys_rows * heads + hid),
        ),
    )(span_order, key_span, latents, modulation.transpose(1, 0, 2), qkv_weight, out_weight, up_weight, down_weight)
    return mixed.reshape(span_count, tok, width).transpose(1, 0, 2)


def fits(nz, ns, tok, span_count, width, head_cols, hid):
    rows = tok * span_count
    total = rows * nz
    keys_rows = ns * total
    weights = 2 * width * (4 * head_cols + 2 * hid) - 2 * width * 3 * head_cols
    moving = 2 * (9 * total * width + 2 * (keys_rows + total) * head_cols)
    moving += 6 * total * keys_rows * (head_cols // HD) + 4 * total * head_cols
    return (
        ns == 8
        and nz > 1
        and rows % 16 == 0
        and tok % 8 == 0
        and head_cols == BLOCK
        and width == hid
        and width == CHUNKS * BLOCK
        and weights + moving < VMEM_BYTES
    )


def body(nz, ns, latents, span_order, modulation, qkv_weight, out_weight, up_weight, down_weight):
    args = (latents, span_order, modulation, qkv_weight, out_weight, up_weight, down_weight)
    if fits(nz, ns, *latents.shape, qkv_weight.shape[2], up_weight.shape[1]):
        return kernel_body(nz, ns, *args)
    return plain_body(*args)


def solution(mesh):
    return jax.shard_map(
        functools.partial(body, mesh.shape["space"], mesh.shape["span"]),
        mesh=mesh,
        in_specs=(
            P("space", "span", None),
            P(),
            P("span", None, None),
            P(None, None, "space"),
            P("space", None),
            P(None, "space"),
            P("space", None),
        ),
        out_specs=P("space", "span", None),
        check_vma=False,
    )
```

```python
import functools

import jax
import jax.numpy as jnp
import numpy as np
from jax import lax
from jax.experimental import pallas as pl
from jax.experimental.pallas import tpu as pltpu
from jax.sharding import PartitionSpec as P

HD = 128
CHUNKS = 6
BLOCK = 512
MESH = pl.DeviceIdType.MESH
VMEM_BYTES = 62 * 1024 * 1024


def norm_mod(rows, shift, scale):
    mean = jnp.mean(rows, axis=-1, keepdims=True)
    centred = rows - mean
    variance = jnp.mean(centred * centred, axis=-1, keepdims=True)
    return (centred * lax.rsqrt(variance + 1e-06) * (1.0 + scale) + shift).astype(jnp.bfloat16)


def plain_body(latents, span_order, modulation, qkv_weight, out_weight, up_weight, down_weight):
    span_count = latents.shape[1]
    head_count = qkv_weight.shape[2] // HD
    my_start = lax.axis_index("span") * span_count
    my_places = lax.dynamic_slice_in_dim(span_order, my_start, span_count, 0)
    gathered = lax.all_gather(latents, "space", axis=0, tiled=True)
    group_rows = gathered.shape[0]
    gathered_f = gathered.astype(jnp.float32)
    normed = norm_mod(gathered_f, modulation[None, :, 0], modulation[None, :, 1])
    projected = jnp.einsum(
        "tcd,sdf->stcf", normed, qkv_weight, preferred_element_type=jnp.float32
    ).astype(jnp.bfloat16)
    query = projected[0].reshape(group_rows, span_count, head_count, HD)
    factor = 1.0 / HD**0.5
    running = jnp.full((head_count, span_count, group_rows), -1e30, jnp.float32)
    key_piece = lax.all_gather(projected[1], "span", axis=1, tiled=True)
    value_piece = lax.all_gather(projected[2], "span", axis=1, tiled=True)
    piece_spans = key_piece.shape[1]
    key_four = key_piece.reshape(group_rows, piece_spans, head_count, HD)
    value_four = value_piece.reshape(group_rows, piece_spans, head_count, HD)
    allowed = (span_order[None, :] <= my_places[:, None])[None, :, None, :, None]
    scores = (
        jnp.einsum("tahd,ubhd->hatbu", query, key_four, preferred_element_type=jnp.float32) * factor
    )
    scores = jnp.where(allowed, scores, -1e30)
    newest = jnp.maximum(running, jnp.max(scores, axis=(3, 4)))
    expo = jnp.where(allowed, jnp.exp(scores - newest[..., None, None]), 0.0)
    denom = jnp.sum(expo, axis=(3, 4))
    accum = jnp.einsum(
        "hatbu,ubhd->hatd",
        expo.astype(jnp.bfloat16),
        value_four,
        preferred_element_type=jnp.float32,
    )
    running, denom, accum = (newest, denom, accum)
    attended = (
        (accum / denom[..., None])
        .transpose(2, 1, 0, 3)
        .reshape(group_rows, span_count, head_count * HD)
        .astype(jnp.bfloat16)
    )
    rows = attended
    attn_sum = lax.psum_scatter(
        jnp.einsum("tck,kd->tcd", rows, out_weight, preferred_element_type=jnp.float32).astype(
            jnp.bfloat16
        ),
        "space",
        scatter_dimension=0,
        tiled=True,
    ).astype(jnp.float32)
    residual = (latents.astype(jnp.float32) + modulation[None, :, 2] * attn_sum).astype(
        jnp.bfloat16
    )
    second = norm_mod(
        lax.all_gather(residual, "space", axis=0, tiled=True).astype(jnp.float32),
        modulation[None, :, 3],
        modulation[None, :, 4],
    )
    hidden = jax.nn.gelu(
        jnp.einsum("tcd,df->tcf", second, up_weight, preferred_element_type=jnp.float32),
        approximate=True,
    ).astype(jnp.bfloat16)
    rows = hidden
    ffn_sum = lax.psum_scatter(
        jnp.einsum("tcf,fd->tcd", rows, down_weight, preferred_element_type=jnp.float32).astype(
            jnp.bfloat16
        ),
        "space",
        scatter_dimension=0,
        tiled=True,
    ).astype(jnp.float32)
    return (residual.astype(jnp.float32) + modulation[None, :, 5] * ffn_sum).astype(jnp.bfloat16)


def flip(index, bit):
    return index + bit * (1 - 2 * ((index // bit) % 2))


def layer_kernel(
    nz, ns, span_count, order_ref, key_span_ref, latent_ref, mod_ref, qkv_hbm, out_hbm, up_hbm, down_hbm,
    mixed_ref,
    x_ref, w_a, w_b, w_out, w_up, gathered, normed, query, kv, expo, scores, denom, attended, part,
    from_left, from_right, from_left2, from_right2, resid, hidden, acc, key_order_ref,
    w_sem, ag_send, ag_recv, kv_send, kv_recv, rs_send, rs_recv,
):
    z = lax.axis_index("space")
    me = lax.axis_index("span")
    rows, width = x_ref.shape
    whole = pl.ds(0, rows)
    tok = rows // span_count
    wide = width // CHUNKS
    last = nz - 1
    heads = query.shape[2] // HD
    down_blocks = width // BLOCK
    first_blocks = w_b.shape[0]

    def load(src, dst, slot):
        return pltpu.make_async_copy(src, dst, w_sem.at[slot])

    def columns(c, size):
        return pl.ds(c * size if isinstance(c, int) else pl.multiple_of(c * size, size), size)

    qkv_loads = [load(qkv_hbm.at[i], w_a.at[i], i) for i in range(3)]
    out_load = load(out_hbm, w_out, 3)
    up_loads = [load(up_hbm.at[:, columns(i, BLOCK)], w_up.at[i], 4 + i) for i in range(w_up.shape[0])]
    down_base = 4 + w_up.shape[0]
    down_loads = [
        load(
            down_hbm.at[:, columns(i, BLOCK)],
            w_b.at[i] if i < first_blocks else w_a.at[i - first_blocks],
            down_base + i,
        )
        for i in range(down_blocks)
    ]
    for i in (1, 2, 0):
        qkv_loads[i].start()
    stored = latent_ref[...].astype(jnp.float32)
    x_ref[...] = jnp.concatenate([stored[:, a, :] for a in range(span_count)], axis=0).astype(jnp.bfloat16)

    barrier = pltpu.get_barrier_semaphore()
    for bit in (1, 2, 4):
        pl.semaphore_signal(barrier, inc=1, device_id=(flip(me, bit), z), device_id_type=MESH)

    @pl.when(z > 0)
    def _():
        pl.semaphore_signal(barrier, inc=1, device_id=(me, z - 1), device_id_type=MESH)

    @pl.when(z < last)
    def _():
        pl.semaphore_signal(barrier, inc=1, device_id=(me, z + 1), device_id_type=MESH)

    pl.semaphore_wait(barrier, 3 + jnp.where(z > 0, 1, 0) + jnp.where(z < last, 1, 0))

    def ag_copy(which, way, s, c, src, dst):
        return pltpu.make_async_remote_copy(
            src_ref=src, dst_ref=dst,
            send_sem=ag_send.at[which, way, s, c], recv_sem=ag_recv.at[which, way, s, c],
            device_id=(me, z + 1 if way == 0 else z - 1), device_id_type=MESH,
        )

    def ag_sends(way, s):
        return jnp.logical_and(z < last, z - s >= 0) if way == 0 else jnp.logical_and(z > 0, z + s <= last)

    def ag_gets(way, s):
        return z - 1 - s >= 0 if way == 0 else z + 1 + s <= last

    def ag_own(which, own, buf, c, at):
        for way in range(2):
            @pl.when(ag_sends(way, 0))
            def _():
                ag_copy(
                    which, way, 0, c, own.at[at, columns(c, wide)], buf.at[z, at, columns(c, wide)]
                ).start()

    def ag_step(which, buf, s, c, at):
        for way in range(2):
            block = z - 1 - s if way == 0 else z + 1 + s

            @pl.when(ag_gets(way, s))
            def _():
                piece = buf.at[block, at, columns(c, wide)]
                ag_copy(which, way, s, c, piece, piece).wait_recv()

            if s + 1 < last:
                @pl.when(ag_sends(way, s + 1))
                def _():
                    piece = buf.at[block, at, columns(c, wide)]
                    ag_copy(which, way, s + 1, c, piece, piece).start()

    def ag_drain(which, buf, at):
        @pl.loop(0, CHUNKS)
        def _(c):
            for way in range(2):
                for s in range(last):
                    @pl.when(ag_sends(way, s))
                    def _():
                        piece = buf.at[0, at, columns(c, wide)]
                        ag_copy(which, way, s, c, piece, piece).wait_send()

    def segments(at):
        first, end = at.start, at.start + at.size
        runs = []
        for a in range(span_count):
            low, high = max(first, a * tok), min(end, (a + 1) * tok)
            if low < high:
                runs.append((a, low - first, high - first))
        return runs

    def norm_block(block, first, at):
        r = block.astype(jnp.float32)
        centred = r - jnp.mean(r, axis=-1, keepdims=True)
        variance = jnp.mean(centred * centred, axis=-1, keepdims=True)
        y = centred * lax.rsqrt(variance + 1e-06)
        pieces = []
        for a, low, high in segments(at):
            shift = mod_ref[first, a : a + 1, :]
            scale = mod_ref[first + 1, a : a + 1, :]
            pieces.append(y[low:high] * (1.0 + scale) + shift)
        return jnp.concatenate(pieces, axis=0).astype(jnp.bfloat16)

    def flip_all(index, rel):
        for bit in (1, 2, 4):
            if rel & bit:
                index = flip(index, bit)
        return index

    def kv_copy(which, rel, bit, block):
        piece = kv.at[which, flip_all(me, rel ^ bit), block]
        return pltpu.make_async_remote_copy(
            src_ref=piece, dst_ref=piece,
            send_sem=kv_send.at[which, rel, block], recv_sem=kv_recv.at[which, rel, block],
            device_id=(flip(me, bit), z), device_id_type=MESH,
        )

    def kv_take(which, rel, block):
        piece = kv.at[which, flip_all(me, rel), block]
        pltpu.make_async_remote_copy(
            src_ref=piece, dst_ref=piece,
            send_sem=kv_send.at[which, rel, block], recv_sem=kv_recv.at[which, rel, block],
            device_id=(flip(me, 1), z), device_id_type=MESH,
        ).wait_recv()

    def project(block, source, first):
        rows_in = norm_block(source, 0, whole)

        def part_of(i):
            if first:
                qkv_loads[i].wait()
            return jnp.dot(rows_in, w_a[i], preferred_element_type=jnp.float32).astype(jnp.bfloat16)

        for which in range(2):
            kv[which, me, block] = part_of(1 + which)
            for bit in ((2, 4, 1), (4, 2, 1))[which]:
                kv_copy(which, bit, bit, block).start()
        normed[block] = rows_in

    def second_hop(block):
        kv_take(0, 2, block)
        kv_copy(0, 6, 4, block).start()
        kv_copy(0, 3, 1, block).start()
        kv_take(1, 4, block)
        kv_copy(1, 6, 2, block).start()
        kv_copy(1, 5, 1, block).start()
        kv_take(0, 4, block)
        kv_copy(0, 5, 1, block).start()
        kv_take(1, 2, block)
        kv_copy(1, 3, 1, block).start()

    def third_hop(block):
        for which in range(2):
            kv_take(which, 6, block)
            kv_copy(which, 7, 1, block).start()

    def each_block(s, do):
        if s == -1:
            do(z)
        elif s >= 0:
            for way in range(2):
                @pl.when(ag_gets(way, s))
                def _():
                    do(z - 1 - s if way == 0 else z + 1 + s)

    @pl.loop(0, CHUNKS)
    def _(c):
        ag_own(0, x_ref, gathered, c, whole)

    out_load.start()
    for copy in up_loads:
        copy.start()
    for copy in down_loads[:first_blocks]:
        copy.start()
    project(z, x_ref[...], True)
    for s in range(last):
        @pl.loop(0, CHUNKS)
        def _(c):
            ag_step(0, gathered, s, c, whole)

        each_block(s, lambda block: project(block, gathered[block], False))
        each_block(s - 1, second_hop)
        each_block(s - 2, third_hop)
    each_block(last - 1, second_hop)
    qkv_loads[0].wait()
    query[...] = (
        jnp.dot(normed[...].reshape(nz * rows, width), w_a[0], preferred_element_type=jnp.float32)
        .astype(jnp.bfloat16)
        .reshape(query.shape)
    )
    for copy in down_loads[first_blocks:]:
        copy.start()
    each_block(last - 2, third_hop)
    each_block(last - 1, third_hop)

    @pl.loop(0, nz)
    def _(block):
        for which in range(2):
            for rel in (1, 3, 5, 7):
                kv_take(which, rel, block)

    total_rows = nz * rows
    keys_rows = ns * total_rows
    factor = 1.0 / HD**0.5
    places = [order_ref[me * span_count + a] for a in range(span_count)]

    key_order = jnp.zeros((1, keys_rows), jnp.int32)
    for span in range(ns * span_count):
        key_order = jnp.where(key_span_ref[...] == span, order_ref[span], key_order)
    key_order_ref[...] = key_order

    def head_scores(h):
        lanes = pl.ds(h * HD, HD)
        keys = kv[0, :, :, :, lanes].reshape(keys_rows, HD)
        scores[h] = lax.dot_general(
            query[:, :, lanes].reshape(total_rows, HD), keys, (((1,), (1,)), ((), ())), preferred_element_type=jnp.float32
        )

    def head_softmax(h):
        key_order = key_order_ref[...]
        for block in range(nz):
            out = []
            sums = []
            for a in range(span_count):
                at = block * rows + a * tok
                allowed = key_order <= places[a]
                sc = jnp.where(allowed, scores[h, at : at + tok, :] * factor, -1e30)
                e = jnp.exp(sc - jnp.max(sc, axis=-1, keepdims=True))
                e = jnp.where(allowed, e, 0.0)
                out.append(e)
                sums.append(jnp.broadcast_to(jnp.sum(e, axis=-1, keepdims=True), (tok, HD)))
            expo[h, block * rows : (block + 1) * rows, :] = jnp.concatenate(out, axis=0).astype(jnp.bfloat16)
            denom[h, block * rows : (block + 1) * rows, :] = jnp.concatenate(sums, axis=0)

    def head_values(h):
        lanes = pl.ds(h * HD, HD)
        mixed_values = jnp.dot(
            expo[h], kv[1, :, :, :, lanes].reshape(keys_rows, HD), preferred_element_type=jnp.float32
        )
        attended[:, lanes] = (mixed_values / denom[h]).astype(jnp.bfloat16)

    head_scores(0)
    for h in range(heads):
        if h + 1 < heads:
            head_scores(h + 1)
        head_softmax(h)
        if h > 0:
            head_values(h - 1)
    head_values(heads - 1)

    def rs_buf(stage, way):
        return ((from_left, from_right), (from_left2, from_right2))[stage][way]

    def rs_copy(stage, way, s, c, owner):
        return pltpu.make_async_remote_copy(
            src_ref=part.at[owner, :, columns(c, wide)],
            dst_ref=rs_buf(stage, way).at[owner, :, columns(c, wide)],
            send_sem=rs_send.at[stage, way, s, c], recv_sem=rs_recv.at[stage, way, s, c],
            device_id=(me, z + 1 if way == 0 else z - 1), device_id_type=MESH,
        )

    def rs_start(stage, c):
        @pl.when(z == 0)
        def _():
            for s in range(last):
                rs_copy(stage, 0, s, c, last - s).start()

        @pl.when(z == last)
        def _():
            for s in range(last):
                rs_copy(stage, 1, s, c, s).start()

    def live(c):
        return jnp.logical_and(c >= 0, c < CHUNKS)

    def farther(at):
        return jnp.where(2 * at > last, at, last - at)

    def rs_tick(stage, t, then):
        for way in range(2):
            c = t + 1 - z if way == 0 else t + 1 - last + z
            inner = z > 0 if way == 0 else z < last
            for s in range(last):
                owner = last - s if way == 0 else s
                beyond = owner > z if way == 0 else owner < z

                @pl.when(jnp.logical_and(jnp.logical_and(inner, beyond), live(c)))
                def _():
                    cols = columns(c, wide)
                    copy = rs_copy(stage, way, s, c, owner)
                    copy.wait_recv()
                    part[owner, :, cols] = (
                        part[owner, :, cols].astype(jnp.float32)
                        + rs_buf(stage, way)[owner, :, cols].astype(jnp.float32)
                    ).astype(jnp.bfloat16)
                    copy.start()

        own = t + 1 - farther(z)

        @pl.when(live(own))
        def _():
            cols = columns(own, wide)
            acc[...] = part[z, :, cols].astype(jnp.float32)

            @pl.when(z > 0)
            def _():
                rs_copy(stage, 0, last - z, own, z).wait_recv()
                acc[...] += rs_buf(stage, 0)[z, :, cols].astype(jnp.float32)

            @pl.when(z < last)
            def _():
                rs_copy(stage, 1, z, own, z).wait_recv()
                acc[...] += rs_buf(stage, 1)[z, :, cols].astype(jnp.float32)

            then(own)

    def rs_drain(stage):
        @pl.loop(0, CHUNKS)
        def _(c):
            for s in range(last):
                for way in range(2):
                    owner = last - s if way == 0 else s

                    @pl.when(owner > z if way == 0 else owner < z)
                    def _():
                        rs_copy(stage, way, s, c, owner).wait_send()

    def ag_tick(t):
        for way in range(2):
            for s in range(last):
                block = z - 1 - s if way == 0 else z + 1 + s
                c = t - farther(block) - s

                @pl.when(jnp.logical_and(ag_gets(way, s), live(c)))
                def _():
                    piece = resid.at[block, :, columns(c, wide)]
                    ag_copy(1, way, s, c, piece, piece).wait_recv()
                    if s + 1 < last:
                        @pl.when(ag_sends(way, s + 1))
                        def _():
                            ag_copy(1, way, s + 1, c, piece, piece).start()

    def gated(base, gate, c):
        base = base.astype(jnp.float32)
        pieces = []
        for a, low, high in segments(whole):
            row = mod_ref[gate, a : a + 1, columns(c, wide)]
            pieces.append(base[low:high] + row * acc[low:high, :])
        return jnp.concatenate(pieces, axis=0).astype(jnp.bfloat16)

    def to_residual(c):
        cols = columns(c, wide)
        resid[z, :, cols] = gated(x_ref[:, cols], 2, c)
        ag_own(1, resid.at[z], resid, c, whole)

    def to_mixed(c):
        cols = columns(c, wide)
        mixed_ref[:, cols] = gated(resid[z, :, cols], 5, c)

    out_load.wait()

    @pl.loop(0, CHUNKS)
    def _(c):
        part[:, :, columns(c, wide)] = (
            jnp.dot(attended[...], w_out[:, columns(c, wide)], preferred_element_type=jnp.float32)
            .astype(jnp.bfloat16)
            .reshape(nz, rows, wide)
        )
        rs_start(0, c)

    @pl.loop(0, CHUNKS + 2 * last - 1)
    def _(t):
        rs_tick(0, t, to_residual)
        ag_tick(t)

    @pl.loop(0, nz)
    def _(block):
        normed[block] = norm_block(resid[block], 3, whole)

    for copy in up_loads:
        copy.wait()

    for i in range(w_up.shape[0]):
        raised = jnp.dot(
            normed[...].reshape(total_rows, width), w_up[i], preferred_element_type=jnp.float32
        )
        hidden[:, columns(i, BLOCK)] = jax.nn.gelu(raised, approximate=True).astype(jnp.bfloat16)

    rs_drain(0)
    for i in range(down_blocks):
        down_loads[i].wait()
        weight = w_b[i] if i < first_blocks else w_a[i - first_blocks]
        part[:, :, columns(i, BLOCK)] = (
            jnp.dot(hidden[...], weight, preferred_element_type=jnp.float32)
            .astype(jnp.bfloat16)
            .reshape(nz, rows, BLOCK)
        )
        rs_start(1, i)
        if i > 0:
            rs_tick(1, i - 1, to_mixed)

    @pl.loop(CHUNKS - 1, CHUNKS + last - 1)
    def _(t):
        rs_tick(1, t, to_mixed)

    rs_drain(1)
    ag_drain(0, gathered, whole)
    ag_drain(1, resid, whole)

    @pl.loop(0, nz)
    def _(block):
        for which in range(2):
            for rel in range(1, 8):
                bit = rel & -rel if rel != 6 else (4 if which == 0 else 2)
                kv_copy(which, rel, bit, block).wait_send()


def kernel_body(nz, ns, latents, span_order, modulation, qkv_weight, out_weight, up_weight, down_weight):
    tok, span_count, width = latents.shape
    rows = tok * span_count
    total = rows * nz
    head_cols = qkv_weight.shape[2]
    heads = head_cols // HD
    hid = up_weight.shape[1]
    keys_rows = ns * total
    key_span = np.broadcast_to(
        np.arange(ns * span_count, dtype=np.int32).reshape(ns, 1, span_count, 1), (ns, nz, span_count, tok)
    ).reshape(1, keys_rows)
    blocks = width // BLOCK
    later = qkv_weight.shape[0]
    bf, f32 = jnp.bfloat16, jnp.float32
    vmem = pl.BlockSpec(memory_space=pltpu.VMEM)
    hbm = pl.BlockSpec(memory_space=pl.ANY)
    grouped = pltpu.VMEM((nz, rows, width), bf)
    flops = 2 * total * width * (4 * head_cols + 2 * hid) + 4 * total * keys_rows * head_cols
    mixed = pl.pallas_call(
        functools.partial(layer_kernel, nz, ns, span_count),
        out_shape=jax.ShapeDtypeStruct((rows, width), bf),
        in_specs=[pl.BlockSpec(memory_space=pltpu.SMEM), vmem, vmem, vmem, hbm, hbm, hbm, hbm],
        out_specs=vmem,
        scratch_shapes=[
            pltpu.VMEM((rows, width), bf),
            pltpu.VMEM((later, width, head_cols), bf),
            pltpu.VMEM((blocks - later, hid, BLOCK), bf),
            pltpu.VMEM((head_cols, width), bf),
            pltpu.VMEM((hid // BLOCK, width, BLOCK), bf),
            grouped,
            grouped,
            pltpu.VMEM((nz, rows, head_cols), bf),
            pltpu.VMEM((2, ns, nz, rows, head_cols), bf),
            pltpu.VMEM((heads, total, keys_rows), bf),
            pltpu.VMEM((heads, total, keys_rows), f32),
            pltpu.VMEM((heads, total, HD), f32),
            pltpu.VMEM((total, head_cols), bf),
            grouped,
            grouped,
            grouped,
            grouped,
            grouped,
            grouped,
            pltpu.VMEM((total, hid), bf),
            pltpu.VMEM((rows, width // CHUNKS), f32),
            pltpu.VMEM((1, keys_rows), jnp.int32),
            pltpu.SemaphoreType.DMA((4 + hid // BLOCK + blocks,)),
            pltpu.SemaphoreType.DMA((2, 2, nz - 1, CHUNKS)),
            pltpu.SemaphoreType.DMA((2, 2, nz - 1, CHUNKS)),
            pltpu.SemaphoreType.DMA((2, ns, nz)),
            pltpu.SemaphoreType.DMA((2, ns, nz)),
            pltpu.SemaphoreType.DMA((2, 2, nz - 1, CHUNKS)),
            pltpu.SemaphoreType.DMA((2, 2, nz - 1, CHUNKS)),
        ],
        compiler_params=pltpu.CompilerParams(
            collective_id=0, has_side_effects=True, vmem_limit_bytes=VMEM_BYTES
        ),
        cost_estimate=pl.CostEstimate(
            flops=flops,
            bytes_accessed=2 * width * (4 * head_cols + 2 * hid),
            transcendentals=total * (keys_rows * heads + hid),
        ),
    )(span_order, key_span, latents, modulation.transpose(1, 0, 2), qkv_weight, out_weight, up_weight, down_weight)
    return mixed.reshape(span_count, tok, width).transpose(1, 0, 2)


def fits(nz, ns, tok, span_count, width, head_cols, hid):
    rows = tok * span_count
    total = rows * nz
    keys_rows = ns * total
    weights = 2 * width * (4 * head_cols + 2 * hid) - 2 * width * 3 * head_cols
    moving = 2 * (9 * total * width + 2 * (keys_rows + total) * head_cols)
    moving += 6 * total * keys_rows * (head_cols // HD) + 4 * total * head_cols
    return (
        ns == 8
        and nz > 1
        and rows % 16 == 0
        and tok % 8 == 0
        and head_cols == BLOCK
        and width == hid
        and width == CHUNKS * BLOCK
        and weights + moving < VMEM_BYTES
    )


def body(nz, ns, latents, span_order, modulation, qkv_weight, out_weight, up_weight, down_weight):
    args = (latents, span_order, modulation, qkv_weight, out_weight, up_weight, down_weight)
    if fits(nz, ns, *latents.shape, qkv_weight.shape[2], up_weight.shape[1]):
        return kernel_body(nz, ns, *args)
    return plain_body(*args)


def solution(mesh):
    return jax.shard_map(
        functools.partial(body, mesh.shape["space"], mesh.shape["span"]),
        mesh=mesh,
        in_specs=(
            P("space", "span", None),
            P(),
            P("span", None, None),
            P(None, None, "space"),
            P("space", None),
            P(None, "space"),
            P("space", None),
        ),
        out_specs=P("space", "span", None),
        check_vma=False,
    )
```
